128 devices in a mesh: fsdp: 8 (over z, core), dp: 16 (over x, y).
Axes of the slice: x: 4, y: 4, z: 4, core: 2. Of those that a mesh axis runs over, the one named last changes fastest.
Arguments:
- gradient: float32 [8192, 8192], P(('fsdp', 'dp')), may hold values from -6 to 6
- moment: float32 [8192, 8192], P(('fsdp', 'dp')), may hold values from -6 to 6
- second: float32 [8192, 8192], P(('fsdp', 'dp')), may hold values from 0.01 to 0.1
- statistics: float32 [128, 1024, 1024], P(('fsdp', 'dp')), as said below
- inv_roots: float32 [128, 1024, 1024], P(('fsdp', 'dp')), as said below
- owner_table: int32 [8, 8], P('fsdp'), may hold values from 0 to 7, each once within a row
Outputs:
- update: float32 [8192, 8192], P(('fsdp', 'dp'))
- new_moment: float32 [8192, 8192], P(('fsdp', 'dp'))
- new_second: float32 [8192, 8192], P(('fsdp', 'dp'))
- new_statistics: float32 [128, 1024, 1024], P(('fsdp', 'dp'))
The draws below stay inside these ranges and needn't reach their ends.
Inputs may be any that keep to these rules, and one draw needn't show every extreme that they name: Each row of owner_table is a permutation of the 8 column blocks. `statistics`: every slot's matrix is symmetric. `inv_roots`: every slot's matrix is symmetric.
All inputs are finite; a program needn't handle non-finite values.
Results may differ from the reference program's by a relative error of at most 0.000075.
Values sent between devices are 32-bit elements; how exact they have to be, the bound alone decides.
No kernel may reach another device: no remote copies, remote signals or barrier semaphores. Data moves between devices by JAX's collectives and lax.ppermute only.
A program may use at most 128 MiB of HBM per device.

```python
import math
import jax
import jax.numpy as jnp
from jax import lax

B = 1024
COLS = 8192
CBLK = 8
ROWS = 8192
BPP = 1
SLOTS = 128
N_FSDP = 8
N_DP = 16


def symmetric_draw(key, count, size, low, high, spread):
    noise_key, diag_key = jax.random.split(key)
    noise = jax.random.normal(noise_key, (count, size, size), jnp.float32) * spread
    noise = (noise + jnp.swapaxes(noise, 1, 2)) * 0.7071
    diagonal = jnp.exp(jax.random.uniform(diag_key, (count, size), jnp.float32, math.log(low), math.log(high)))
    identity = jnp.eye(size, dtype=jnp.float32)
    return noise * (1.0 - identity) + diagonal[:, :, None] * identity


def draw_statistics(key, part):
    key = jax.random.fold_in(key, 1)
    return symmetric_draw(key, SLOTS, B, 300.0, 3000.0, 20.0)


def draw_inv_roots(key, part):
    key = jax.random.fold_in(key, 2)
    return symmetric_draw(key, SLOTS, B, 0.08, 0.3, 0.004)


def block_scale(stream_key, dims, cuts, smallest, high):
    factor_of, own = 1.0, jax.random.fold_in(stream_key, 6)
    for axis_at, parts in cuts:
        heights = jnp.exp(jax.random.uniform(jax.random.fold_in(own, axis_at), (parts,), jnp.float32, smallest / len(cuts), high / len(cuts)))
        factor_of = factor_of * jnp.repeat(heights, dims[axis_at] // parts).reshape([-1 if axis == axis_at else 1 for axis in range(len(dims))])
    return factor_of


def bell_draw(rng, shape, scale, reach, cuts=(), held_as=jnp.bfloat16):
    values = scale * jax.random.normal(rng, shape, jnp.float32)
    if cuts:
        values = values * block_scale(rng, shape, cuts, -0.22, 0.18)
    return jnp.clip(values, -reach, reach).astype(held_as)


def setup_inputs(seed: int = 0) -> dict:
    seeds = jax.random.split(jax.random.key(seed), 7)
    gradient = bell_draw(seeds[0], (ROWS, COLS), 1.0, 6.0, ((0, 128),), jnp.float32)
    moment = bell_draw(seeds[1], (ROWS, COLS), 1.0, 6.0, ((0, 128),), jnp.float32)
    second = jnp.clip(jnp.exp(math.log(0.1) - 2.3025851 * jax.random.uniform(seeds[2], (ROWS, COLS), jnp.float32) ** block_scale(seeds[2], (ROWS, COLS), ((0, 128),), -0.2, 0.2)), 0.01, 0.1)
    statistics = draw_statistics(jax.random.fold_in(seeds[6], 71), 0)
    inv_roots = draw_inv_roots(jax.random.fold_in(seeds[6], 71), 0)
    owner_table = jax.vmap(lambda own: jax.random.permutation(own, CBLK))(jax.random.split(seeds[5], N_FSDP)).reshape((N_FSDP, CBLK)).astype(jnp.int32)
    return {"gradient": gradient, "moment": moment, "second": second, "statistics": statistics, "inv_roots": inv_roots, "owner_table": owner_table}


BETA_STAT = 0.95
BETA_ONE = 0.9
BETA_TWO = 0.999
BIAS_ONE = 1.0 - 0.9 ** 10
BIAS_TWO = 1.0 - 0.999 ** 10
ADAM_EPS = 1e-08
CLIP_RMS = 0.25
PRECISE = lax.Precision.HIGHEST

def reference(gradient, moment, second, statistics, inv_roots, owner_table):
    col_blocks = COLS // B
    blocks = gradient.reshape(N_FSDP, B, col_blocks, B).transpose(0, 2, 1, 3).reshape(N_FSDP * col_blocks, B, B)
    fsdp_rows = jnp.arange(N_FSDP, dtype=jnp.int32)[:, None]
    placed = owner_table.astype(jnp.int32)
    left_idx = ((fsdp_rows * N_DP + 2 * (placed // BPP)) * BPP + placed % BPP).reshape(-1).astype(jnp.int32)
    right_idx = (left_idx + BPP).astype(jnp.int32)

    def per_block(item):
        block_grad, left_slot, right_slot = item
        left_stat = BETA_STAT * statistics[left_slot] + (1.0 - BETA_STAT) * jnp.dot(block_grad, block_grad.T, precision=PRECISE)
        right_stat = BETA_STAT * statistics[right_slot] + (1.0 - BETA_STAT) * jnp.dot(block_grad.T, block_grad, precision=PRECISE)
        shaped = jnp.dot(jnp.dot(inv_roots[left_slot], block_grad, precision=PRECISE), inv_roots[right_slot], precision=PRECISE)
        return (left_stat, right_stat, shaped)
    left_new, right_new, precond = lax.map(per_block, (blocks, left_idx, right_idx))
    new_statistics = jnp.zeros_like(statistics).at[left_idx].set(left_new).at[right_idx].set(right_new)
    new_moment = BETA_ONE * moment + (1.0 - BETA_ONE) * gradient
    new_second = BETA_TWO * second + (1.0 - BETA_TWO) * gradient * gradient
    adam_step = new_moment / BIAS_ONE / (jnp.sqrt(new_second / BIAS_TWO) + ADAM_EPS)
    adam_sq = lax.optimization_barrier(jnp.sum((adam_step * adam_step).reshape(N_FSDP, B, col_blocks, B), axis=(1, 3))).reshape(-1)
    prec_sq = lax.optimization_barrier(jnp.sum(precond * precond, axis=(1, 2)))
    ratio = jnp.sqrt(adam_sq / (prec_sq + 1e-06))
    total = jnp.sum(adam_sq)
    clip = jnp.minimum(1.0, CLIP_RMS * math.sqrt(gradient.shape[0] * gradient.shape[1]) / jnp.sqrt(total + 1e-06))
    grafted = precond * (ratio * clip)[:, None, None]
    update = grafted.reshape(N_FSDP, col_blocks, B, B).transpose(0, 2, 1, 3).reshape(N_FSDP * B, COLS)
    return (update, new_moment, new_second, new_statistics)
```

```python
import math

import jax
import jax.numpy as jnp
from jax import lax
from jax.experimental import pallas as pl
from jax.experimental.pallas import tpu as pltpu
from jax.sharding import PartitionSpec as P

BETA_STAT = 0.95
BETA_ONE = 0.9
BETA_TWO = 0.999
BIAS_ONE = 1.0 - 0.9**10
BIAS_TWO = 1.0 - 0.999**10
ADAM_EPS = 1e-08
CLIP_RMS = 0.25
SPLIT = lax.Precision.HIGH
SIDE = 4


def route(move):
    pairs = []
    for src in range(SIDE * SIDE):
        x, y = move(src // SIDE, src % SIDE)
        pairs.append((src, (x % SIDE) * SIDE + y % SIDE))
    return pairs


NEAR = route(lambda x, y: (x, y ^ 1))
FAR = route(lambda x, y: (x, 3 - y))
GROUPS = [
    [SIDE * x + y for x in range(SIDE) for y in (0, 3)],
    [SIDE * x + y for x in range(SIDE) for y in (1, 2)],
]


def near(v):
    return lax.ppermute(v, "dp", NEAR)


def far(v):
    return lax.ppermute(v, "dp", FAR)


def along_x(v, shift):
    return lax.ppermute(v, "dp", route(lambda x, y: (x + shift, y)))


def swap(v, axis, bit):
    count = lax.axis_size(axis)
    return lax.ppermute(v, axis, [(i, i ^ bit) for i in range(count)])


def dot(a, b, a_dim=1, b_dim=0):
    return lax.dot_general(
        a, b, (((a_dim,), (b_dim,)), ((), ())), precision=SPLIT, preferred_element_type=jnp.float32
    )


def take_columns(gradient, cols, order):
    rows, count = gradient.shape[0], cols.shape[0]

    def body(cols_ref, g_ref, out_ref):
        out_ref[0] = g_ref[...]

    return pl.pallas_call(
        body,
        grid_spec=pltpu.PrefetchScalarGridSpec(
            num_scalar_prefetch=1,
            grid=(count,),
            in_specs=[pl.BlockSpec((rows, order), lambda k, cols_ref: (0, cols_ref[k]))],
            out_specs=pl.BlockSpec((1, rows, order), lambda k, cols_ref: (k, 0, 0)),
        ),
        out_shape=jax.ShapeDtypeStruct((count, rows, order), jnp.float32),
        cost_estimate=pl.CostEstimate(
            flops=0, bytes_accessed=8 * count * rows * order, transcendentals=0
        ),
    )(cols, gradient)


def place_columns(pieces, source, scale):
    count, rows, order = pieces.shape

    def body(source_ref, scale_ref, p_ref, out_ref):
        out_ref[...] = p_ref[0] * scale_ref[pl.program_id(0)]

    return pl.pallas_call(
        body,
        grid_spec=pltpu.PrefetchScalarGridSpec(
            num_scalar_prefetch=2,
            grid=(count,),
            in_specs=[
                pl.BlockSpec((1, rows, order), lambda k, source_ref, scale_ref: (source_ref[k], 0, 0))
            ],
            out_specs=pl.BlockSpec((rows, order), lambda k, source_ref, scale_ref: (0, k)),
        ),
        out_shape=jax.ShapeDtypeStruct((rows, count * order), jnp.float32),
        cost_estimate=pl.CostEstimate(
            flops=count * rows * order, bytes_accessed=8 * count * rows * order, transcendentals=0
        ),
    )(source, scale, pieces)


def pack_symmetric(mat):
    half = mat.shape[0] // 2
    row = lax.broadcasted_iota(jnp.int32, (half, half), 0)
    col = lax.broadcasted_iota(jnp.int32, (half, half), 1)
    both = jnp.where(row <= col, mat[:half, :half], mat[half:, half:])
    diag = jnp.sum(jnp.where(row == col, mat[half:, half:], 0.0), axis=0)
    last = jnp.zeros((8, 2 * half), jnp.float32).at[0, :half].set(diag)
    return jnp.concatenate([jnp.concatenate([mat[:half, half:], both], axis=1), last], axis=0)


def unpack_symmetric(packed):
    half = packed.shape[1] // 2
    row = lax.broadcasted_iota(jnp.int32, (half, half), 0)
    col = lax.broadcasted_iota(jnp.int32, (half, half), 1)
    cross, both, diag = packed[:half, :half], packed[:half, half:], packed[half, :half]
    top = jnp.where(row <= col, both, both.T)
    low = jnp.where(row > col, both, jnp.where(row == col, diag[:, None], both.T))
    return jnp.concatenate(
        [jnp.concatenate([top, cross], axis=1), jnp.concatenate([cross.T, low], axis=1)], axis=0
    )


def local(gradient, moment, second, statistics, inv_roots, owner_table):
    rows_dev, width = gradient.shape
    order = statistics.shape[1]
    col_blocks = width // order
    half = order // 2
    place = lax.axis_index("dp")
    x, y = place // SIDE, place % SIDE
    is_left = y % 2 == 0
    high = y // 2
    outer = (y == 0) | (y == 3)

    owner_row = owner_table[0]
    positions = jnp.arange(col_blocks, dtype=jnp.int32)
    column_of = jnp.sum(
        jnp.where(owner_row[None, :] == positions[:, None], positions[None, :], 0), axis=1
    )

    root = inv_roots[0]
    root_rows = root.reshape(SIDE, SIDE, rows_dev, order)
    rows_outer = jnp.concatenate([root_rows[:, 0:1], root_rows[:, 3:4]], axis=1).reshape(half, order)
    rows_inner = root_rows[:, 1:3].reshape(half, order)
    sent_rows = jnp.pad(jnp.where(outer, rows_inner, rows_outer), ((0, 8), (0, 0)))
    got = near(jnp.where(is_left, sent_rows, pack_symmetric(root)))

    shift = jnp.arange(SIDE, dtype=jnp.int32)[:, None]
    other = jnp.arange(2, dtype=jnp.int32)[None, :]
    send_pos = 2 * ((x + shift) % SIDE) + (high ^ other)
    outgoing = take_columns(gradient, column_of[send_pos.reshape(-1)], order)
    outgoing = outgoing.reshape(SIDE, 2, rows_dev, order)
    arrived = [outgoing[0]] + [along_x(outgoing[d], d) for d in range(1, SIDE)]
    own_y = [v[0] for v in arrived]
    far_y = [far(v[1]) for v in arrived]
    near_own = [near(v) for v in own_y]
    near_far = [near(v) for v in far_y]
    block = jnp.zeros((SIDE, SIDE, rows_dev, order), jnp.float32)
    for pieces, from_y in ((own_y, y), (far_y, 3 - y), (near_own, y ^ 1), (near_far, 3 - (y ^ 1))):
        for d in range(SIDE):
            block = lax.dynamic_update_slice(
                block, pieces[d][None, None], ((x - d) % SIDE, from_y, 0, 0)
            )
    block = block.reshape(order, order)

    new_moment = BETA_ONE * moment + (1.0 - BETA_ONE) * gradient
    new_second = BETA_TWO * second + (1.0 - BETA_TWO) * gradient * gradient
    adam_step = new_moment / BIAS_ONE / (jnp.sqrt(new_second / BIAS_TWO) + ADAM_EPS)
    squares = jnp.sum((adam_step * adam_step).reshape(rows_dev, col_blocks, order), axis=(0, 2))
    for bit in (4, 8, 3, 1):
        squares = squares + swap(squares, "dp", bit)
    total = jnp.broadcast_to(jnp.sum(squares), squares.shape)
    for bit in (1, 2, 4):
        total = total + swap(total, "fsdp", bit)

    own_rows = jnp.where(outer, rows_outer, rows_inner)
    left_rows = jnp.where(is_left, own_rows, got[:half])
    right_mat = lax.cond(is_left, lambda: unpack_symmetric(got), lambda: root)
    shaped = dot(dot(left_rows, block), right_mat)
    sum_sq = jnp.sum(shaped * shaped)
    sums = lax.all_to_all(
        jnp.broadcast_to(sum_sq, (SIDE * SIDE, 8, 128)), "dp", 0, 0, tiled=True
    )[:, 0, 0]
    pieces = lax.all_to_all(
        shaped.reshape(2 * SIDE, rows_dev, order),
        "dp",
        0,
        0,
        axis_index_groups=GROUPS,
        tiled=True,
    )

    stat = statistics[0]
    new_stat = lax.cond(
        is_left,
        lambda: BETA_STAT * stat + (1.0 - BETA_STAT) * dot(block, block, 1, 1),
        lambda: BETA_STAT * stat + (1.0 - BETA_STAT) * dot(block, block, 0, 0),
    )

    prec_sq = jnp.sum(sums.reshape(col_blocks, 2), axis=1)[owner_row]
    ratio = jnp.sqrt(squares / (prec_sq + 1e-06))
    count_all = order * lax.axis_size("fsdp") * width
    clip = jnp.minimum(1.0, CLIP_RMS * math.sqrt(count_all) / jnp.sqrt(total + 1e-06))
    update = place_columns(pieces, owner_row, ratio * clip)
    return (update, new_moment, new_second, new_stat[None])


def solution(mesh):
    placed = (
        P(("fsdp", "dp"), None),
        P(("fsdp", "dp"), None),
        P(("fsdp", "dp"), None),
        P(("fsdp", "dp"), None, None),
        P(("fsdp", "dp"), None, None),
        P("fsdp", None),
    )
    return jax.shard_map(
        local,
        mesh=mesh,
        in_specs=placed,
        out_specs=(
            P(("fsdp", "dp"), None),
            P(("fsdp", "dp"), None),
            P(("fsdp", "dp"), None),
            P(("fsdp", "dp"), None, None),
        ),
        check_vma=False,
    )
```

```python
import math

import jax
import jax.numpy as jnp
from jax import lax
from jax.experimental import pallas as pl
from jax.experimental.pallas import tpu as pltpu
from jax.sharding import PartitionSpec as P

BETA_STAT = 0.95
BETA_ONE = 0.9
BETA_TWO = 0.999
BIAS_ONE = 1.0 - 0.9**10
BIAS_TWO = 1.0 - 0.999**10
ADAM_EPS = 1e-08
CLIP_RMS = 0.25
SIDE = 4


def route(move):
    pairs = []
    for src in range(SIDE * SIDE):
        x, y = move(src // SIDE, src % SIDE)
        pairs.append((src, (x % SIDE) * SIDE + y % SIDE))
    return pairs


NEAR = route(lambda x, y: (x, y ^ 1))
FAR = route(lambda x, y: (x, 3 - y))
VMEM_BYTES = 56 * 2**20
GROUPS = [
    [SIDE * x + y for x in range(SIDE) for y in (0, 3)],
    [SIDE * x + y for x in range(SIDE) for y in (1, 2)],
]


def near(v):
    return lax.ppermute(v, "dp", NEAR)


def far(v):
    return lax.ppermute(v, "dp", FAR)


def along_x(v, shift):
    return lax.ppermute(v, "dp", route(lambda x, y: (x + shift, y)))


def swap(v, axis, bit):
    count = lax.axis_size(axis)
    return lax.ppermute(v, axis, [(i, i ^ bit) for i in range(count)])

ANY = pl.BlockSpec(memory_space=pl.ANY)
VMEM = pl.BlockSpec(memory_space=pltpu.VMEM)
SMEM = pl.BlockSpec(memory_space=pltpu.SMEM)


def call(body, out, in_specs, out_specs, scratch, flops, moved):
    return pl.pallas_call(
        body,
        out_shape=out,
        in_specs=in_specs,
        out_specs=out_specs,
        scratch_shapes=scratch,
        compiler_params=pltpu.CompilerParams(vmem_limit_bytes=VMEM_BYTES),
        cost_estimate=pl.CostEstimate(flops=flops, bytes_accessed=moved, transcendentals=0),
    )


def f32(*shape):
    return jax.ShapeDtypeStruct(shape, jnp.float32)


def spot():
    place = lax.axis_index("dp")
    x, y = lax.shift_right_logical(place, 2), lax.bitwise_and(place, 3)
    is_left = lax.bitwise_and(y, 1) == 0
    outer = jnp.logical_or(y == 0, y == 3)
    return x, y, is_left, outer


def side_y(outer, g):
    return jnp.where(outer, 3 * g, 1 + g)


def run(copies):
    for copy in copies:
        copy.start()
    return copies


def finish(copies):
    for copy in copies:
        copy.wait()


def split(v):
    high = v.astype(jnp.bfloat16)
    return high, (v - high.astype(jnp.float32)).astype(jnp.bfloat16)


def mul(a, b):
    return jnp.dot(a, b, preferred_element_type=jnp.float32)


def mul_split(a_high, a_low, b_high, b_low):
    return mul(a_high, b_high) + (mul(a_high, b_low) + mul(a_low, b_high))


def cut(gradient, root, owner_table):
    rows, width = gradient.shape
    order = root.shape[0]
    half = order // 2
    count = width // order
    part = rows // 2

    def body(owner_ref, g_ref, root_ref, own_ref, oth_ref, x1_ref, x2_ref, x3_ref, c_ref, sems):
        x, y, is_left, outer = spot()
        outs = [(own_ref, oth_ref)] + [(r.at[0], r.at[1]) for r in (x1_ref, x2_ref, x3_ref)]
        copies = []
        for d in range(SIDE):
            for j in range(2):
                pos = 2 * lax.bitwise_and(x + d, 3) + lax.bitwise_xor(lax.shift_right_logical(y, 1), j)
                col = jnp.int32(0)
                for c in range(count):
                    col = col + jnp.where(owner_ref[0, c] == pos, c, 0)
                copies.append(
                    pltpu.make_async_copy(
                        g_ref.at[:, pl.ds(pl.multiple_of(col * order, order), order)],
                        outs[d][j],
                        sems.at[2 * d + j],
                    )
                )
        run(copies)

        @pl.when(is_left)
        def _():
            sent = []
            for k in range(2 * SIDE):
                row = ((k // 2) * SIDE + side_y(jnp.logical_not(outer), k % 2)) * rows
                sent.append(
                    pltpu.make_async_copy(
                        root_ref.at[pl.ds(pl.multiple_of(row, rows), part), :],
                        c_ref.at[pl.ds(k * part, part), :],
                        sems.at[2 * SIDE + k],
                    )
                )
            finish(run(sent))

        @pl.when(jnp.logical_not(is_left))
        def _():
            finish(
                run(
                    [
                        pltpu.make_async_copy(
                            root_ref.at[pl.ds(h * half // 2, half // 2), pl.ds(half, half)],
                            c_ref.at[:, pl.ds(h * half, half)],
                            sems.at[2 * SIDE + h],
                        )
                        for h in range(2)
                    ]
                )
            )

        finish(copies)

    return call(
        body,
        [f32(rows, order)] * 2 + [f32(2, rows, order)] * 3 + [f32(half // 2, order)],
        [SMEM, ANY, ANY],
        [ANY] * 6,
        [pltpu.SemaphoreType.DMA((4 * SIDE,))],
        0,
        24 * rows * width,
    )(owner_table, gradient, root)


def pack(root, rows, which, *after):
    order = root.shape[0]
    half, quarter = order // 2, order // 4
    part = rows // 4

    def body(root_ref, *refs):
        out_ref, buf, sems = refs[len(after) :]
        x, y, is_left, outer = spot()
        body_rows = 2 * SIDE * part
        out_ref[body_rows:, :] = jnp.zeros((8, order), jnp.float32)

        @pl.when(is_left)
        def _():
            sent = []
            for k in range(2 * SIDE):
                row = ((k // 2) * SIDE + side_y(jnp.logical_not(outer), k % 2)) * rows
                row = row + rows // 2 + which * part
                sent.append(
                    pltpu.make_async_copy(
                        root_ref.at[pl.ds(pl.multiple_of(row, part), part), :],
                        out_ref.at[pl.ds(k * part, part), :],
                        sems.at[k],
                    )
                )
            finish(run(sent))

        @pl.when(jnp.logical_not(is_left))
        def _():
            at = pl.ds(which * half, half)
            finish(run([pltpu.make_async_copy(root_ref.at[at, at], buf, sems.at[0])]))
            row = lax.broadcasted_iota(jnp.int32, (quarter, quarter), 0)
            col = lax.broadcasted_iota(jnp.int32, (quarter, quarter), 1)
            low = buf[quarter:, quarter:]
            both = jnp.where(row <= col, buf[:quarter, :quarter], low)
            mid = quarter // 2
            for h in range(2):
                out_ref[:body_rows, h * half : h * half + quarter] = buf[h * mid : (h + 1) * mid, quarter:]
                out_ref[:body_rows, h * half + quarter : (h + 1) * half] = both[h * mid : (h + 1) * mid]
            out_ref[body_rows : body_rows + 1, :quarter] = jnp.sum(
                jnp.where(row == col, low, 0.0), axis=0, keepdims=True
            )

    return call(
        body,
        f32(2 * SIDE * part + 8, order),
        [ANY] * (1 + len(after)),
        VMEM,
        [pltpu.VMEM((half, half), jnp.float32), pltpu.SemaphoreType.DMA((2 * SIDE,))],
        0,
        4 * half * order,
    )(root, *after)


def first_product(pieces, root):
    rows, order = pieces[0].shape
    half, tile = order // 2, order // 4
    count = len(pieces)

    def body(*refs):
        piece_refs, root_ref = refs[:count], refs[count]
        g_out, high_ref, low_ref, g_buf, r_buf, g_high, g_low, r_high, r_low, sems = refs[count + 1 :]
        x, y, is_left, outer = spot()
        from_y = (y, 3 - y, lax.bitwise_xor(y, 1), 3 - lax.bitwise_xor(y, 1))
        copies = []
        for k in range(count):
            row = (lax.bitwise_and(x - k % SIDE, 3) * SIDE + from_y[k // SIDE]) * rows
            copies.append(
                pltpu.make_async_copy(
                    piece_refs[k], g_buf.at[pl.ds(pl.multiple_of(row, rows), rows), :], sems.at[k]
                )
            )
        run(copies)

        def cut_two(src, high, low, first, last):
            def step(i, carry):
                at = pl.ds(pl.multiple_of(i * 64, 64), 64)
                a, b = split(src[at, :])
                high[at, :] = a
                low[at, :] = b
                return carry

            lax.fori_loop(first, last, step, 0)

        @pl.when(is_left)
        def _():
            sent = []
            for k in range(2 * SIDE):
                row = ((k // 2) * SIDE + side_y(outer, k % 2)) * rows
                sent.append(
                    pltpu.make_async_copy(
                        root_ref.at[pl.ds(pl.multiple_of(row, rows), rows), :],
                        r_buf.at[pl.ds(k * rows, rows), :],
                        sems.at[count + k],
                    )
                )
            finish(run(sent))
            cut_two(r_buf, r_high, r_low, 0, half // 64)

        @pl.when(jnp.logical_not(is_left))
        def _():
            finish(run([pltpu.make_async_copy(root_ref, r_buf, sems.at[count])]))
            cut_two(r_buf, r_high, r_low, 0, order // 64)

        finish(copies)
        out = pltpu.make_async_copy(g_buf, g_out, sems.at[0])
        out.start()
        cut_two(g_buf, g_high, g_low, 0, order // 64)

        def product(a_high, a_low, b_high, b_low, tiles):
            def step(i, carry):
                at = pl.ds(pl.multiple_of(i * tile, tile), tile)
                for n in range(2):
                    cols = slice(n * half, (n + 1) * half)
                    acc = mul_split(a_high[at, :], a_low[at, :], b_high[:, cols], b_low[:, cols])
                    high_ref[at, cols], low_ref[at, cols] = split(acc)
                return carry

            lax.fori_loop(0, tiles, step, 0)

        @pl.when(is_left)
        def _():
            product(r_high, r_low, g_high, g_low, 2)

        @pl.when(jnp.logical_not(is_left))
        def _():
            product(g_high, g_low, r_high, r_low, 4)

        out.wait()

    part = jax.ShapeDtypeStruct((order, order), jnp.bfloat16)
    whole = pltpu.VMEM((order, order), jnp.float32)
    short = pltpu.VMEM((order, order), jnp.bfloat16)
    return call(
        body,
        [f32(order, order), part, part],
        [ANY] * (count + 1),
        [ANY, VMEM, VMEM],
        [whole, whole, short, short, short, short, pltpu.SemaphoreType.DMA((count + 2 * SIDE,))],
        6 * order**3,
        16 * order * order,
    )(*pieces, root)


def unfold(c_ref, b_high, b_low, base):
    half = c_ref.shape[1] // 2
    quarter = half // 2
    mid = quarter // 2
    row = lax.broadcasted_iota(jnp.int32, (quarter, quarter), 0)
    col = lax.broadcasted_iota(jnp.int32, (quarter, quarter), 1)
    cross = jnp.concatenate([c_ref[:mid, :quarter], c_ref[:mid, half : half + quarter]], axis=0)
    both = jnp.concatenate([c_ref[:mid, quarter:half], c_ref[:mid, half + quarter :]], axis=0)
    diag = c_ref[mid : mid + 1, :quarter]
    turned = both.T
    top = jnp.where(row <= col, both, turned)
    low = jnp.where(row > col, both, jnp.where(row == col, diag, turned))
    for r, left_mat, right_mat in ((0, top, cross), (1, cross.T, low)):
        at = slice(base + r * quarter, base + (r + 1) * quarter)
        b_high[at, :quarter], b_low[at, :quarter] = split(left_mat)
        b_high[at, quarter:], b_low[at, quarter:] = split(right_mat)


def second_product(which, t_high, t_low, chunks, squares):
    order = t_high.shape[0]
    half, quarter = order // 2, order // 4
    dests = 2 * SIDE
    part = quarter // dests
    count = len(chunks)

    def body(high_ref, low_ref, *refs):
        chunk_refs, sq_ref = refs[:count], refs[count]
        out_ref, sq_out, b_high, b_low = refs[count + 1 :]
        x, y, is_left, outer = spot()

        @pl.when(is_left)
        def _():
            c_ref = chunk_refs[0]
            if which == 0:
                unfold(chunk_refs[1], b_high, b_low, 0)
                for h in range(2):
                    cols = slice(h * quarter, (h + 1) * quarter)
                    turned = c_ref[:, h * half : (h + 1) * half].T
                    b_high[half:, cols], b_low[half:, cols] = split(turned)
            else:
                for h in range(2):
                    at = slice(h * quarter, (h + 1) * quarter)
                    b_high[at, :], b_low[at, :] = split(c_ref[:, h * half : (h + 1) * half])
                unfold(chunk_refs[2], b_high, b_low, half)
            total = jnp.float32(0.0)
            for m in range(2):
                at = slice(m * quarter, (m + 1) * quarter)
                acc = mul_split(high_ref[at, :], low_ref[at, :], b_high[...], b_low[...])
                total = total + jnp.sum(acc * acc)
                for k in range(SIDE):
                    for h in range(2):
                        first = (2 * k + h) * part
                        out_ref[m * SIDE + k, :, h * half : (h + 1) * half] = acc[first : first + part]
            sq_out[...] = sq_ref[...] + total

        @pl.when(jnp.logical_not(is_left))
        def _():
            if which == 0:
                a = chunk_refs[0][...]
            else:
                a = jnp.concatenate([chunk_refs[1][: quarter // 2], chunk_refs[2][: quarter // 2]], axis=0)
            a_high, a_low = split(a)
            total = jnp.float32(0.0)
            for n in range(2):
                cols = slice(n * half, (n + 1) * half)
                acc = mul_split(a_high, a_low, high_ref[:, cols], low_ref[:, cols])
                total = total + jnp.sum(acc * acc)
                for k in range(dests):
                    if which == 0:
                        out_ref[k, :, cols] = acc[k * part : (k + 1) * part]
                    else:
                        few = part // 2
                        out_ref[k, :few, cols] = acc[k * few : (k + 1) * few]
                        out_ref[k, few:, cols] = acc[quarter // 2 + k * few : quarter // 2 + (k + 1) * few]
            sq_out[...] = sq_ref[...] + total

    short = pltpu.VMEM((order, half), jnp.bfloat16)
    return call(
        body,
        [f32(dests, part, order), f32(8, 128)],
        [VMEM] * (3 + count),
        [VMEM, VMEM],
        [short, short],
        3 * order**3 // 2,
        10 * order * order,
    )(t_high, t_low, *chunks, squares)


def update_statistics(block, stat, after):
    order = block.shape[0]
    tile = order // 4
    tiles = order // tile

    def body(g_ref, s_ref, after_ref, out_ref, high, low):
        x, y, is_left, outer = spot()

        @pl.when(is_left)
        def _():
            for i in range(tiles):
                at = slice(i * tile, (i + 1) * tile)
                high[at, :], low[at, :] = split(g_ref[at, :])

        @pl.when(jnp.logical_not(is_left))
        def _():
            for i in range(tiles):
                for j in range(tiles):
                    at, cols = slice(i * tile, (i + 1) * tile), slice(j * tile, (j + 1) * tile)
                    high[at, cols], low[at, cols] = split(g_ref[cols, at].T)

        def outer_mul(a, b):
            return lax.dot_general(a, b, (((1,), (1,)), ((), ())), preferred_element_type=jnp.float32)

        for i in range(tiles):
            at = slice(i * tile, (i + 1) * tile)
            for j in range(i, tiles):
                to = slice(j * tile, (j + 1) * tile)
                acc = outer_mul(high[at, :], high[to, :]) + (
                    outer_mul(high[at, :], low[to, :]) + outer_mul(low[at, :], high[to, :])
                )
                acc = (1.0 - BETA_STAT) * acc
                out_ref[at, to] = BETA_STAT * s_ref[at, to] + acc
                if i != j:
                    out_ref[to, at] = BETA_STAT * s_ref[to, at] + acc.T

    short = pltpu.VMEM((order, order), jnp.bfloat16)
    return call(
        body,
        f32(order, order),
        [VMEM, VMEM, ANY],
        VMEM,
        [short, short],
        4 * order**3,
        12 * order * order,
    )(block, stat, after)


def place_columns(first, second, owner_table, scale):
    count, part, order = first.shape
    half = order // 2

    def body(owner_ref, scale_ref, first_ref, second_ref, out_ref):
        x, y, is_left, outer = spot()
        for c in range(count):
            p = owner_ref[0, c]
            s = scale_ref[c]
            from_left = (lax.bitwise_and(p, 1) == 0) == outer
            a, b = first_ref[p, :, :half], first_ref[p, :, half:]
            d, e = second_ref[p, :, :half], second_ref[p, :, half:]
            out_ref[:part, c * order : c * order + half] = a * s
            out_ref[:part, c * order + half : (c + 1) * order] = jnp.where(from_left, d, b) * s
            out_ref[part:, c * order : c * order + half] = jnp.where(from_left, b, d) * s
            out_ref[part:, c * order + half : (c + 1) * order] = e * s

    return call(
        body,
        f32(2 * part, count * order),
        [SMEM, SMEM, VMEM, VMEM],
        VMEM,
        [],
        count * part * order,
        16 * count * part * order,
    )(owner_table, scale, first, second)


def sent_back(v):
    return lax.all_to_all(v, "dp", 0, 0, axis_index_groups=GROUPS, tiled=True)


def local(gradient, moment, second, statistics, inv_roots, owner_table):
    rows_dev, width = gradient.shape
    order = statistics.shape[1]
    col_blocks = width // order
    root = inv_roots[0]

    own, oth, x1, x2, x3, chunk = cut(gradient, root, owner_table)
    near_own = [near(own)]
    chunk_a = near(chunk)
    far_y = [far(oth)]
    own_y = [own]
    for d, v in ((1, x1), (3, x3), (2, x2)):
        arrived = along_x(v, d)
        own_y.append(arrived[0])
        far_y.append(far(arrived[1]))
    near_far = [near(far_y[0])]
    for d in range(1, SIDE):
        near_own.append(near(own_y[d]))
        near_far.append(near(far_y[d]))

    new_moment = BETA_ONE * moment + (1.0 - BETA_ONE) * gradient
    new_second = BETA_TWO * second + (1.0 - BETA_TWO) * gradient * gradient
    adam_step = new_moment / BIAS_ONE / (jnp.sqrt(new_second / BIAS_TWO) + ADAM_EPS)
    sums = jnp.sum((adam_step * adam_step).reshape(rows_dev, col_blocks, order), axis=(0, 2))
    for bit in (4, 8, 3):
        sums = sums + swap(sums, "dp", bit)
    total = jnp.broadcast_to(jnp.sum(sums), sums.shape)
    bit = 1
    while bit < lax.axis_size("fsdp"):
        total = total + swap(total, "fsdp", bit)
        bit *= 2
    sums = jnp.stack([sums, total])

    chunk_b = near(pack(root, rows_dev, 0, near_far[1], sums))
    chunk_c = near(pack(root, rows_dev, 1, near_far[2]))
    sums = sums + swap(sums, "dp", 1)

    order_d = (0, 1, 3, 2)
    pieces = []
    for group in (own_y, far_y, near_own, near_far):
        by_shift = dict(zip(order_d, group))
        pieces += [by_shift[d] for d in range(SIDE)]
    block, t_high, t_low = first_product(pieces, root)
    half_a, squares = second_product(
        0, t_high, t_low, [chunk_a, chunk_b], jnp.zeros((8, 128), jnp.float32)
    )
    back_a = sent_back(half_a)
    half_b, squares = second_product(1, t_high, t_low, [chunk_a, chunk_b, chunk_c], squares)
    back_b = sent_back(half_b)
    squares = squares + near(squares)
    prec_sq = sent_back(jnp.broadcast_to(squares, (2 * SIDE, 8, 128)))[:, 0, 0]

    new_stat = update_statistics(block, statistics[0], half_b)

    ratio = jnp.sqrt(sums[0] / (prec_sq[owner_table[0]] + 1e-06))
    count_all = order * lax.axis_size("fsdp") * width
    clip = jnp.minimum(1.0, CLIP_RMS * math.sqrt(count_all) / jnp.sqrt(sums[1] + 1e-06))
    update = place_columns(back_a, back_b, owner_table, ratio * clip)
    return (update, new_moment, new_second, new_stat[None])


def solution(mesh):
    placed = (
        P(("fsdp", "dp"), None),
        P(("fsdp", "dp"), None),
        P(("fsdp", "dp"), None),
        P(("fsdp", "dp"), None, None),
        P(("fsdp", "dp"), None, None),
        P("fsdp", None),
    )
    return jax.shard_map(
        local,
        mesh=mesh,
        in_specs=placed,
        out_specs=(
            P(("fsdp", "dp"), None),
            P(("fsdp", "dp"), None),
            P(("fsdp", "dp"), None),
            P(("fsdp", "dp"), None, None),
        ),
        check_vma=False,
    )
```

```python
import math

import jax
import jax.numpy as jnp
from jax import lax
from jax.experimental import pallas as pl
from jax.experimental.pallas import tpu as pltpu
from jax.sharding import PartitionSpec as P

BETA_STAT = 0.95
BETA_ONE = 0.9
BETA_TWO = 0.999
BIAS_ONE = 1.0 - 0.9**10
BIAS_TWO = 1.0 - 0.999**10
ADAM_EPS = 1e-08
CLIP_RMS = 0.25
SIDE = 4


def route(move):
    pairs = []
    for src in range(SIDE * SIDE):
        x, y = move(src // SIDE, src % SIDE)
        pairs.append((src, (x % SIDE) * SIDE + y % SIDE))
    return pairs


NEAR = route(lambda x, y: (x, y ^ 1))
FAR = route(lambda x, y: (x, 3 - y))
GROUPS = [
    [SIDE * x + y for x in range(SIDE) for y in (0, 3)],
    [SIDE * x + y for x in range(SIDE) for y in (1, 2)],
]


def near(v):
    return lax.ppermute(v, "dp", NEAR)


def far(v):
    return lax.ppermute(v, "dp", FAR)


def along_x(v, shift):
    return lax.ppermute(v, "dp", route(lambda x, y: (x + shift, y)))


def tie(v, *after):
    return lax.optimization_barrier((v, *after))[0]


def swap(v, axis, bit):
    count = lax.axis_size(axis)
    return lax.ppermute(v, axis, [(i, i ^ bit) for i in range(count)])

HBM = pl.BlockSpec(memory_space=pltpu.HBM)
VMEM = pl.BlockSpec(memory_space=pltpu.VMEM)
SMEM = pl.BlockSpec(memory_space=pltpu.SMEM)


def call(body, out, in_specs, out_specs, scratch, flops, moved, vmem=16):
    return pl.pallas_call(
        body,
        out_shape=out,
        in_specs=in_specs,
        out_specs=out_specs,
        scratch_shapes=scratch,
        compiler_params=pltpu.CompilerParams(vmem_limit_bytes=vmem * 2**20),
        cost_estimate=pl.CostEstimate(flops=flops, bytes_accessed=moved, transcendentals=0),
    )


def f32(*shape):
    return jax.ShapeDtypeStruct(shape, jnp.float32)


def spot():
    place = lax.axis_index("dp")
    x, y = lax.shift_right_logical(place, 2), lax.bitwise_and(place, 3)
    is_left = lax.bitwise_and(y, 1) == 0
    outer = jnp.logical_or(y == 0, y == 3)
    return x, y, is_left, outer


def rows_of(k, x, y, rows):
    return (lax.bitwise_and(x + k // 2, 3) * SIDE + (3 - y if k % 2 else y)) * rows


def run(copies):
    for copy in copies:
        copy.start()
    return copies


def finish(copies):
    for copy in copies:
        copy.wait()


def split(v):
    high = v.astype(jnp.bfloat16)
    return high, (v - high.astype(jnp.float32)).astype(jnp.bfloat16)


def mul(a, b):
    return jnp.dot(a, b, preferred_element_type=jnp.float32)


def mul_split(a_high, a_low, b_high, b_low):
    return mul(a_high, b_high) + (mul(a_high, b_low) + mul(a_low, b_high))


def unit_copies(root_ref, unit, rows, x, y, is_left, to_ref, sems, base):
    few = rows // 4
    copies = []
    for k in range(2 * SIDE):
        row = rows_of(k, x, lax.bitwise_xor(y, 1), rows) + unit * few
        copies.append(
            pltpu.make_async_copy(
                root_ref.at[pl.ds(pl.multiple_of(row, few), few), :],
                to_ref.at[pl.ds(k * few, few), :],
                sems.at[base + k],
            )
        )
    return copies


def cross_copies(root_ref, unit, to_ref, sems, base):
    order = root_ref.shape[0]
    half, part = order // 2, order // 8
    return [
        pltpu.make_async_copy(
            root_ref.at[pl.ds((2 * unit + h) * part, part), pl.ds(half, half)],
            to_ref.at[:, pl.ds(h * half, half)],
            sems.at[base + h],
        )
        for h in range(2)
    ]


def column_of(owner_ref, pos, count):
    col = jnp.int32(0)
    for c in range(count):
        col = col + jnp.where(owner_ref[0, c] == pos, c, 0)
    return col


def position(x, y, d, j):
    return 2 * lax.bitwise_and(x + d, 3) + lax.bitwise_xor(lax.shift_right_logical(y, 1), j)


def cut(gradient, root, owner_table):
    rows, width = gradient.shape
    order = root.shape[0]
    count = width // order
    part = order // 8

    def body(owner_ref, g_ref, root_ref, lead_ref, oth_ref, x1_ref, x2_ref, x3_ref, sems):
        x, y, is_left, outer = spot()
        outs = [(lead_ref.at[pl.ds(part, rows), :], oth_ref)]
        outs += [(r.at[pl.ds(0, rows), :], r.at[pl.ds(rows, rows), :]) for r in (x1_ref, x2_ref, x3_ref)]
        copies = []
        for d in range(SIDE):
            for j in range(2):
                col = column_of(owner_ref, position(x, y, d, j), count)
                at = pl.ds(pl.multiple_of(col * order, order), order)
                copies.append(pltpu.make_async_copy(g_ref.at[:, at], outs[d][j], sems.at[2 * d + j]))
        run(copies)
        chunk_ref = lead_ref.at[pl.ds(0, part), :]

        @pl.when(is_left)
        def _():
            finish(run(unit_copies(root_ref, 0, rows, x, y, is_left, chunk_ref, sems, 2 * SIDE)))

        @pl.when(jnp.logical_not(is_left))
        def _():
            finish(run(cross_copies(root_ref, 0, chunk_ref, sems, 2 * SIDE)))

        finish(copies)

    return call(
        body,
        [f32(part + rows, order), f32(rows, order)] + [f32(2 * rows, order)] * 3,
        [SMEM, HBM, HBM],
        [VMEM] * 5,
        [pltpu.SemaphoreType.DMA((4 * SIDE,))],
        0,
        8 * rows * width,
        60,
    )(owner_table, gradient, root)


def adam(gradient, moment, second, order):
    rows, width = gradient.shape
    count = width // order

    def body(g_ref, m_ref, s_ref, m_out, s_out, sums_ref):
        for c in range(count):
            cols = slice(c * order, (c + 1) * order)

            def step(i, total):
                at = pl.ds(pl.multiple_of(i * 8, 8), 8)
                g = g_ref[at, cols]
                new_m = BETA_ONE * m_ref[at, cols] + (1.0 - BETA_ONE) * g
                new_s = BETA_TWO * s_ref[at, cols] + (1.0 - BETA_TWO) * g * g
                m_out[at, cols] = new_m
                s_out[at, cols] = new_s
                a = new_m / BIAS_ONE / (jnp.sqrt(new_s / BIAS_TWO) + ADAM_EPS)
                return total + a * a

            total = lax.fori_loop(0, rows // 8, step, jnp.zeros((8, order), jnp.float32))
            sums_ref[c : c + 1, :] = jnp.sum(total, axis=0, keepdims=True)

    return call(
        body,
        [f32(rows, width)] * 2 + [f32(8, order)],
        [VMEM] * 3,
        [VMEM] * 3,
        [],
        0,
        24 * rows * width,
    )(gradient, moment, second)


def pack(root, rows, units):
    order = root.shape[0]
    half, quarter, part = order // 2, order // 4, order // 8
    fold = units[-1]
    last = (len(units) - 1) * part

    def body(root_ref, out_ref, buf, sems):
        x, y, is_left, outer = spot()
        out_ref[last + part :, :] = jnp.zeros((8, order), jnp.float32)

        @pl.when(is_left)
        def _():
            copies = []
            for i, unit in enumerate(units):
                to_ref = out_ref.at[pl.ds(i * part, part), :]
                copies += unit_copies(root_ref, unit, rows, x, y, is_left, to_ref, sems, 2 * SIDE * i)
            finish(run(copies))

        @pl.when(jnp.logical_not(is_left))
        def _():
            at = pl.ds((fold - 2) * half, half)
            copies = [pltpu.make_async_copy(root_ref.at[at, at], buf, sems.at[0])]
            for i, unit in enumerate(units[:-1]):
                to_ref = out_ref.at[pl.ds(i * part, part), :]
                copies += cross_copies(root_ref, unit, to_ref, sems, 2 * i + 1)
            finish(run(copies))
            row = lax.broadcasted_iota(jnp.int32, (quarter, quarter), 0)
            col = lax.broadcasted_iota(jnp.int32, (quarter, quarter), 1)
            low = buf[quarter:, quarter:]
            both = jnp.where(row <= col, buf[:quarter, :quarter], low)
            at = slice(last, last + part)
            for h in range(2):
                out_ref[at, h * half : h * half + quarter] = buf[h * part : (h + 1) * part, quarter:]
                out_ref[at, h * half + quarter : (h + 1) * half] = both[h * part : (h + 1) * part]
            out_ref[last + part : last + part + 1, :quarter] = jnp.sum(
                jnp.where(row == col, low, 0.0), axis=0, keepdims=True
            )

    return call(
        body,
        f32(last + part + 8, order),
        [HBM],
        VMEM,
        [pltpu.VMEM((half, half), jnp.float32), pltpu.SemaphoreType.DMA((2 * SIDE * len(units),))],
        0,
        8 * len(units) * part * order,
    )(root)


def in_vmem(*shape):
    return pltpu.VMEM(shape, jnp.bfloat16)


def cut_two(src, high, low, tiles):
    def step(i, carry):
        at = pl.ds(pl.multiple_of(i * 64, 64), 64)
        high[at, :], low[at, :] = split(src[at, :])
        return carry

    lax.fori_loop(0, tiles, step, 0)


def split_root(root, rows):
    order = root.shape[0]

    def body(root_ref, high_ref, low_ref, buf, sems):
        x, y, is_left, outer = spot()

        @pl.when(is_left)
        def _():
            copies = []
            for k in range(2 * SIDE):
                row = rows_of(k, x, y, rows)
                copies.append(
                    pltpu.make_async_copy(
                        root_ref.at[pl.ds(pl.multiple_of(row, rows), rows), :],
                        buf.at[pl.ds(k * rows, rows), :],
                        sems.at[k],
                    )
                )
            finish(run(copies))
            cut_two(buf, high_ref, low_ref, order // 128)

        @pl.when(jnp.logical_not(is_left))
        def _():
            finish(run([pltpu.make_async_copy(root_ref, buf, sems.at[0])]))
            cut_two(buf, high_ref, low_ref, order // 64)

    return call(
        body,
        [in_vmem(order, order)] * 2,
        [HBM],
        [VMEM, VMEM],
        [pltpu.VMEM((order, order), jnp.float32), pltpu.SemaphoreType.DMA((2 * SIDE,))],
        0,
        8 * order * order,
    )(root)


def first_product(pieces, rows, r_high, r_low):
    order = r_high.shape[0]
    half, tile = order // 2, order // 4
    count = len(pieces)

    def body(*refs):
        piece_refs, (rh_ref, rl_ref) = refs[:count], refs[count : count + 2]
        gh_ref, gl_ref, high_ref, low_ref, buf, sems = refs[count + 2 :]
        x, y, is_left, outer = spot()
        from_y = (y, 3 - y, lax.bitwise_xor(y, 1), 3 - lax.bitwise_xor(y, 1))
        copies = []
        for k in range(count):
            row = (lax.bitwise_and(x - k % SIDE, 3) * SIDE + from_y[k // SIDE]) * rows
            copies.append(
                pltpu.make_async_copy(
                    piece_refs[k].at[pl.ds(pieces[k][1], rows), :],
                    buf.at[pl.ds(pl.multiple_of(row, rows), rows), :],
                    sems.at[k],
                )
            )
        finish(run(copies))
        cut_two(buf, gh_ref, gl_ref, order // 64)

        def product(a_high, a_low, b_high, b_low, tiles):
            def step(i, carry):
                at = pl.ds(pl.multiple_of(i * tile, tile), tile)
                for n in range(2):
                    cols = slice(n * half, (n + 1) * half)
                    acc = mul_split(a_high[at, :], a_low[at, :], b_high[:, cols], b_low[:, cols])
                    high_ref[at, cols], low_ref[at, cols] = split(acc)
                return carry

            lax.fori_loop(0, tiles, step, 0)

        @pl.when(is_left)
        def _():
            product(rh_ref, rl_ref, gh_ref, gl_ref, 2)

        @pl.when(jnp.logical_not(is_left))
        def _():
            product(gh_ref, gl_ref, rh_ref, rl_ref, 4)

    return call(
        body,
        [in_vmem(order, order)] * 4,
        [HBM] * count + [VMEM] * 2,
        [VMEM] * 4,
        [pltpu.VMEM((order, order), jnp.float32), pltpu.SemaphoreType.DMA((count,))],
        0,
        order * order,
    )(*(piece for piece, _ in pieces), r_high, r_low)


def unfold(c_ref, first, b_high, b_low, base):
    half = c_ref.shape[1] // 2
    quarter = half // 2
    mid = quarter // 2
    row = lax.broadcasted_iota(jnp.int32, (quarter, quarter), 0)
    col = lax.broadcasted_iota(jnp.int32, (quarter, quarter), 1)
    at = slice(first, first + mid)
    cross = jnp.concatenate([c_ref[at, :quarter], c_ref[at, half : half + quarter]], axis=0)
    both = jnp.concatenate([c_ref[at, quarter:half], c_ref[at, half + quarter :]], axis=0)
    diag = c_ref[first + mid : first + mid + 1, :quarter]
    turned = both.T
    top = jnp.where(row <= col, both, turned)
    low = jnp.where(row > col, both, jnp.where(row == col, diag, turned))
    for r, left_mat, right_mat in ((0, top, cross), (1, cross.T, low)):
        at = slice(base + r * quarter, base + (r + 1) * quarter)
        b_high[at, :quarter], b_low[at, :quarter] = split(left_mat)
        b_high[at, quarter:], b_low[at, quarter:] = split(right_mat)


def second_product(which, t_high, t_low, chunks, squares):
    order = t_high.shape[0]
    half, quarter, eighth = order // 2, order // 4, order // 8
    dests = 2 * SIDE
    part = quarter // dests
    few = part // 2
    count = len(chunks)

    def body(high_ref, low_ref, *refs):
        chunk_refs, sq_ref = refs[:count], refs[count]
        whole, sq_out, b_high, b_low = refs[count + 1 :]
        x, y, is_left, outer = spot()
        outs = []
        for k in range(dests):
            to_y = 3 - y if k % 2 else y
            outs.append(whole.at[2 * lax.bitwise_and(x + k // 2, 3) + lax.shift_right_logical(to_y, 1)])
        units = [(chunk_refs[0], 0), (chunk_refs[1], 0), (chunk_refs[1], eighth), (chunk_refs[-1], 0)]

        @pl.when(is_left)
        def _():
            for q in range(4):
                c_ref, first = units[q // 2]
                at = slice(q * eighth, (q + 1) * eighth)
                mat = c_ref[first : first + eighth, (q % 2) * half : (q % 2 + 1) * half]
                if which == 0:
                    b_high[half:, at], b_low[half:, at] = split(mat.T)
                else:
                    b_high[at, :], b_low[at, :] = split(mat)
            unfold(*units[2 + which], b_high, b_low, half * which)
            total = jnp.float32(0.0)
            for m in range(2):
                at = slice(m * quarter, (m + 1) * quarter)
                acc = mul_split(high_ref[at, :], low_ref[at, :], b_high[...], b_low[...])
                total = total + jnp.sum(acc * acc)
                for k in range(SIDE):
                    for h in range(2):
                        first = (2 * k + h) * part
                        for q in range(SIDE):
                            at = slice((h * SIDE + q) * part, (h * SIDE + q + 1) * part)
                            lanes = slice(q * 128, (q + 1) * 128)
                            outs[m * SIDE + k][at, :] = acc[first : first + part, lanes]
            sq_out[...] = sq_ref[...] + total

        @pl.when(jnp.logical_not(is_left))
        def _():
            mats = []
            for c_ref, first in units[2 * which : 2 * which + 2]:
                mats.append(c_ref[first : first + eighth, :])
            a_high, a_low = split(jnp.concatenate(mats, axis=0))
            total = jnp.float32(0.0)
            for n in range(2):
                cols = slice(n * half, (n + 1) * half)
                acc = mul_split(a_high, a_low, high_ref[:, cols], low_ref[:, cols])
                total = total + jnp.sum(acc * acc)
                for k in range(dests):
                    for q in range(SIDE):
                        first = (n * SIDE + q) * part
                        lanes = slice(q * 128, (q + 1) * 128)
                        outs[k][first : first + few, :] = acc[k * few : (k + 1) * few, lanes]
                        outs[k][first + few : first + part, :] = acc[
                            eighth + k * few : eighth + (k + 1) * few, lanes
                        ]
            sq_out[...] = sq_ref[...] + total

        if which == 1:
            for k in range(dests):
                whole[k, 8 * part :, :] = sq_out[...]

    short = pltpu.VMEM((order, half), jnp.bfloat16)
    return call(
        body,
        [f32(dests, 8 * part + 8 * which, 128), f32(8, 128)],
        [VMEM] * (3 + count),
        [VMEM] * 2,
        [short, short],
        0,
        140 * order * order * which,
    )(t_high, t_low, *chunks, squares)


def update_statistics(g_high, g_low, stat):
    order = g_high.shape[0]
    tile = order // 4
    tiles = order // tile

    def body(gh_ref, gl_ref, s_ref, out_ref, zero_ref, high, low):
        x, y, is_left, outer = spot()
        zero_ref[...] = jnp.zeros((8, 128), jnp.float32)

        @pl.when(is_left)
        def _():
            high[...] = gh_ref[...]
            low[...] = gl_ref[...]

        @pl.when(jnp.logical_not(is_left))
        def _():
            for i in range(tiles):
                for j in range(tiles):
                    at, cols = slice(i * tile, (i + 1) * tile), slice(j * tile, (j + 1) * tile)
                    high[at, cols] = gh_ref[cols, at].T
                    low[at, cols] = gl_ref[cols, at].T

        def outer_mul(a, b):
            return lax.dot_general(a, b, (((1,), (1,)), ((), ())), preferred_element_type=jnp.float32)

        for i in range(tiles):
            at = slice(i * tile, (i + 1) * tile)
            for j in range(i, tiles):
                to = slice(j * tile, (j + 1) * tile)
                acc = outer_mul(high[at, :], high[to, :]) + (
                    outer_mul(high[at, :], low[to, :]) + outer_mul(low[at, :], high[to, :])
                )
                acc = (1.0 - BETA_STAT) * acc
                out_ref[at, to] = BETA_STAT * s_ref[at, to] + acc
                if i != j:
                    out_ref[to, at] = BETA_STAT * s_ref[to, at] + acc.T

    short = pltpu.VMEM((order, order), jnp.bfloat16)
    return call(
        body,
        [f32(order, order), f32(8, 128)],
        [VMEM, VMEM, VMEM],
        [VMEM, VMEM],
        [short, short],
        0,
        order * order,
        24,
    )(g_high, g_low, stat)


def place_columns(first, second, ends, sums, totals, owner_table, largest):
    count = first.shape[0]
    part = first.shape[1] // 8
    order = 8 * first.shape[2]
    end = 8 * part

    def body(owner_ref, first_ref, second_ref, ends_ref, sums_ref, totals_ref, out_ref, scratch):
        x, y, is_left, outer = spot()
        total = jnp.sum(jnp.sum(totals_ref[...], axis=0, keepdims=True), axis=1, keepdims=True)
        clip = jnp.minimum(1.0, largest / jnp.sqrt(total + 1e-06))
        scratch[...] = jnp.broadcast_to(jnp.sum(sums_ref[...], axis=1, keepdims=True), (count, 128))
        for k in range(count):
            from_y = 3 - y if k % 2 else y
            p = 2 * lax.bitwise_and(x - k // 2, 3) + lax.shift_right_logical(from_y, 1)
            from_left = lax.bitwise_and(from_y, 1) == 0
            col = column_of(owner_ref, p, count)
            squares = second_ref[p, end : end + 1, :] + ends_ref[p, :1, :]
            scale = jnp.sqrt(scratch[pl.ds(col, 1), :] / (squares + 1e-06)) * clip
            for j in range(8):
                cols = pl.ds(pl.multiple_of(col * order + j * 128, 128), 128)
                at = slice(j * part, (j + 1) * part)
                back = (j + 4) % 8
                across = slice(back * part, (back + 1) * part)
                if j < 4:
                    out_ref[:part, cols] = first_ref[p, at, :] * scale
                    other = jnp.where(from_left, first_ref[p, across, :], second_ref[p, at, :])
                    out_ref[part:, cols] = other * scale
                else:
                    other = jnp.where(from_left, second_ref[p, across, :], first_ref[p, at, :])
                    out_ref[:part, cols] = other * scale
                    out_ref[part:, cols] = second_ref[p, at, :] * scale

    return call(
        body,
        f32(2 * part, count * order),
        [SMEM] + [VMEM] * 5,
        VMEM,
        [pltpu.VMEM((count, 128), jnp.float32)],
        0,
        16 * count * part * order,
    )(owner_table, first, second, ends, sums, totals)


def sent_back(parts):
    return lax.all_to_all(parts, "dp", 0, 0, axis_index_groups=GROUPS, tiled=True)


def local(gradient, moment, second, statistics, inv_roots, owner_table):
    rows_dev, width = gradient.shape
    order = statistics.shape[1]
    root = inv_roots[0]

    lead, oth, x1, x2, x3 = cut(gradient, root, owner_table)
    lead_got = near(lead)
    far_y = {0: far(oth)}
    new_moment, new_second, own_sums = adam(gradient, moment, second, order)
    got_x = {1: along_x(x1, 1), 3: along_x(x3, 3)}
    got_x[2] = along_x(tie(x2, far_y[0], own_sums), 2)
    own_y = {d: got_x[d][:rows_dev] for d in (1, 2, 3)}
    oth_y = {d: got_x[d][rows_dev:] for d in (1, 2, 3)}
    own_sums = tie(own_sums, got_x[2])
    sums = own_sums
    for d in (1, 2, 3):
        sums = sums + along_x(own_sums, d)
    far_y[1] = far(tie(oth_y[1], got_x[3]))
    far_y[3] = far(tie(oth_y[3], got_x[1]))
    far_y[2] = far(jnp.concatenate([oth_y[2], sums], axis=0))
    sums = sums + far_y[2][rows_dev:]

    near_own, near_far = {}, {}
    near_far[0] = near(tie(far_y[0], lead_got))
    near_own[3] = near(tie(own_y[3], near_far[0]))
    near_far[3] = near(tie(far_y[3], near_own[3], got_x[2]))
    near_own[1] = near(tie(own_y[1], lead_got))
    near_far[1] = near(tie(far_y[1], near_own[1]))
    near_own[2] = near(tie(own_y[2], near_far[1], far_y[2]))
    near_far[2] = near(tie(jnp.concatenate([far_y[2][:rows_dev], sums], axis=0), near_far[3]))
    sums = sums + near_far[2][rows_dev:]

    chunk_b = pack(root, rows_dev, (1, 2))
    chunk_c = pack(root, rows_dev, (3,))
    r_high, r_low = split_root(root, rows_dev)
    chunk_b = near(tie(chunk_b, near_own[2], near_far[2]))
    chunk_c = near(tie(chunk_c, near_far[2]))

    lead_rows = lead.shape[0] - rows_dev
    pieces = [(lead, lead_rows)] + [(got_x[d], 0) for d in (1, 2, 3)]
    pieces += [(far_y[d], 0) for d in range(SIDE)]
    pieces += [(lead_got, lead_rows)] + [(near_own[d], 0) for d in (1, 2, 3)]
    pieces += [(near_far[d], 0) for d in range(SIDE)]
    g_high, g_low, t_high, t_low = first_product(pieces, rows_dev, r_high, r_low)
    new_stat, squares = update_statistics(g_high, g_low, statistics[0])
    half_a, squares = second_product(0, t_high, t_low, [lead_got, chunk_b], squares)
    back_a = sent_back(half_a)
    half_b, _ = second_product(1, t_high, t_low, [lead_got, chunk_b, chunk_c], squares)
    back_b = sent_back(tie(half_b, back_a))
    ends = near(back_b[:, half_a.shape[1] :])

    totals = tie(sums, back_a)
    bit = 1
    while bit < lax.axis_size("fsdp"):
        totals = totals + swap(totals, "fsdp", bit)
        bit *= 2

    count_all = order * lax.axis_size("fsdp") * width
    update = place_columns(
        back_a, back_b, ends, sums, totals, owner_table, CLIP_RMS * math.sqrt(count_all)
    )
    return (update, new_moment, new_second, new_stat[None])


def solution(mesh):
    placed = (
        P(("fsdp", "dp"), None),
        P(("fsdp", "dp"), None),
        P(("fsdp", "dp"), None),
        P(("fsdp", "dp"), None, None),
        P(("fsdp", "dp"), None, None),
        P("fsdp", None),
    )
    return jax.shard_map(
        local,
        mesh=mesh,
        in_specs=placed,
        out_specs=(
            P(("fsdp", "dp"), None),
            P(("fsdp", "dp"), None),
            P(("fsdp", "dp"), None),
            P(("fsdp", "dp"), None, None),
        ),
        check_vma=False,
    )
```

```python
import math

import jax
import jax.numpy as jnp
from jax import lax
from jax.experimental import pallas as pl
from jax.experimental.pallas import tpu as pltpu
from jax.sharding import PartitionSpec as P

BETA_STAT = 0.95
BETA_ONE = 0.9
BETA_TWO = 0.999
BIAS_ONE = 1.0 - 0.9**10
BIAS_TWO = 1.0 - 0.999**10
ADAM_EPS = 1e-08
CLIP_RMS = 0.25
SIDE = 4


def route(move):
    pairs = []
    for src in range(SIDE * SIDE):
        x, y = move(src // SIDE, src % SIDE)
        pairs.append((src, (x % SIDE) * SIDE + y % SIDE))
    return pairs


NEAR = route(lambda x, y: (x, y ^ 1))
FAR = route(lambda x, y: (x, 3 - y))
GROUPS = [
    [SIDE * x + y for x in range(SIDE) for y in (0, 3)],
    [SIDE * x + y for x in range(SIDE) for y in (1, 2)],
]


def near(v):
    return lax.ppermute(v, "dp", NEAR)


def far(v):
    return lax.ppermute(v, "dp", FAR)


def along_x(v, shift):
    return lax.ppermute(v, "dp", route(lambda x, y: (x + shift, y)))


def tie(v, *after):
    return lax.optimization_barrier((v, *after))[0]


def swap(v, axis, bit):
    count = lax.axis_size(axis)
    return lax.ppermute(v, axis, [(i, i ^ bit) for i in range(count)])

HBM = pl.BlockSpec(memory_space=pltpu.HBM)
VMEM = pl.BlockSpec(memory_space=pltpu.VMEM)
SMEM = pl.BlockSpec(memory_space=pltpu.SMEM)


def call(body, out, in_specs, out_specs, scratch, flops, moved, vmem=16):
    return pl.pallas_call(
        body,
        out_shape=out,
        in_specs=in_specs,
        out_specs=out_specs,
        scratch_shapes=scratch,
        compiler_params=pltpu.CompilerParams(vmem_limit_bytes=vmem * 2**20),
        cost_estimate=pl.CostEstimate(flops=flops, bytes_accessed=moved, transcendentals=0),
    )


def f32(*shape):
    return jax.ShapeDtypeStruct(shape, jnp.float32)


def spot():
    place = lax.axis_index("dp")
    x, y = lax.shift_right_logical(place, 2), lax.bitwise_and(place, 3)
    is_left = lax.bitwise_and(y, 1) == 0
    outer = jnp.logical_or(y == 0, y == 3)
    return x, y, is_left, outer


def rows_of(k, x, y, rows):
    return (lax.bitwise_and(x + k // 2, 3) * SIDE + (3 - y if k % 2 else y)) * rows


def run(copies):
    for copy in copies:
        copy.start()
    return copies


def finish(copies):
    for copy in copies:
        copy.wait()


def split(v):
    high = v.astype(jnp.bfloat16)
    return high, (v - high.astype(jnp.float32)).astype(jnp.bfloat16)


def mul(a, b):
    return jnp.dot(a, b, preferred_element_type=jnp.float32)


def mul_split(a_high, a_low, b_high, b_low):
    return mul(a_high, b_high) + (mul(a_high, b_low) + mul(a_low, b_high))


def unit_copies(root_ref, unit, rows, x, y, is_left, to_ref, sems, base):
    few = rows // 4
    copies = []
    for k in range(2 * SIDE):
        row = rows_of(k, x, lax.bitwise_xor(y, 1), rows) + unit * few
        copies.append(
            pltpu.make_async_copy(
                root_ref.at[pl.ds(pl.multiple_of(row, few), few), :],
                to_ref.at[pl.ds(k * few, few), :],
                sems.at[base + k],
            )
        )
    return copies


def cross_copies(root_ref, unit, to_ref, sems, base):
    order = root_ref.shape[0]
    half, part = order // 2, order // 8
    return [
        pltpu.make_async_copy(
            root_ref.at[pl.ds((2 * unit + h) * part, part), pl.ds(half, half)],
            to_ref.at[:, pl.ds(h * half, half)],
            sems.at[base + h],
        )
        for h in range(2)
    ]


def column_of(owner_ref, pos, count):
    col = jnp.int32(0)
    for c in range(count):
        col = col + jnp.where(owner_ref[0, c] == pos, c, 0)
    return col


def position(x, y, d, j):
    return 2 * lax.bitwise_and(x + d, 3) + lax.bitwise_xor(lax.shift_right_logical(y, 1), j)


def cut(gradient, root, owner_table):
    rows, width = gradient.shape
    order = root.shape[0]
    count = width // order
    part = order // 8
    sizes = [(part + rows, order), (rows, order)] + [(2 * rows, order)] * 3

    def body(owner_ref, g_ref, root_ref, lead_ref, oth_ref, x1_ref, x2_ref, x3_ref, sems):
        x, y, is_left, outer = spot()
        outs = [(lead_ref.at[pl.ds(part, rows), :], oth_ref)]
        outs += [(r.at[pl.ds(0, rows), :], r.at[pl.ds(rows, rows), :]) for r in (x1_ref, x2_ref, x3_ref)]
        copies = []
        for d in range(SIDE):
            for j in range(2):
                col = column_of(owner_ref, position(x, y, d, j), count)
                at = pl.ds(pl.multiple_of(col * order, order), order)
                copies.append(pltpu.make_async_copy(g_ref.at[:, at], outs[d][j], sems.at[2 * d + j]))
        run(copies)
        chunk_ref = lead_ref.at[pl.ds(0, part), :]

        @pl.when(is_left)
        def _():
            finish(run(unit_copies(root_ref, 0, rows, x, y, is_left, chunk_ref, sems, 2 * SIDE)))

        @pl.when(jnp.logical_not(is_left))
        def _():
            finish(run(cross_copies(root_ref, 0, chunk_ref, sems, 2 * SIDE)))

        finish(copies)

    return call(
        body,
        [in_vmem(*size, dtype=jnp.float32) for size in sizes],
        [SMEM, HBM, HBM],
        [VMEM] * 5,
        [pltpu.SemaphoreType.DMA((4 * SIDE,))],
        0,
        8 * rows * width,
        60,
    )(owner_table, gradient, root)


def adam(gradient, moment, second, order):
    rows, width = gradient.shape
    count = width // order

    def body(g_ref, m_ref, s_ref, m_out, s_out, sums_ref):
        def step(i, total):
            at = pl.ds(pl.multiple_of(i * 8, 8), 8)
            g = g_ref[at, :]
            new_m = BETA_ONE * m_ref[at, :] + (1.0 - BETA_ONE) * g
            new_s = BETA_TWO * s_ref[at, :] + (1.0 - BETA_TWO) * g * g
            m_out[at, :] = new_m
            s_out[at, :] = new_s
            a = new_m / BIAS_ONE / (jnp.sqrt(new_s / BIAS_TWO) + ADAM_EPS)
            return total + a * a

        total = lax.fori_loop(0, rows // 8, step, jnp.zeros((8, 2 * order), jnp.float32))
        total = jnp.sum(total, axis=0, keepdims=True)
        for h in range(2):
            sums_ref[pl.ds(2 * pl.program_id(0) + h, 1), :] = total[:, h * order : (h + 1) * order]

    block = pl.BlockSpec((rows, 2 * order), lambda c: (0, c))
    return pl.pallas_call(
        body,
        grid=(count // 2,),
        out_shape=[f32(rows, width)] * 2 + [f32(8, order)],
        in_specs=[block] * 3,
        out_specs=[block] * 2 + [pl.BlockSpec((8, order), lambda c: (0, 0))],
        compiler_params=pltpu.CompilerParams(vmem_limit_bytes=40 * 2**20),
        cost_estimate=pl.CostEstimate(flops=0, bytes_accessed=24 * rows * width, transcendentals=0),
    )(gradient, moment, second)


def pack(root, rows):
    order = root.shape[0]
    half, quarter, part = order // 2, order // 4, order // 8

    def body(root_ref, b_ref, c_ref, buf, sems):
        x, y, is_left, outer = spot()
        places = [(b_ref, 0), (b_ref, part), (c_ref, 0)]
        for to_ref in (b_ref, c_ref):
            to_ref[to_ref.shape[0] - 8 :, :] = jnp.zeros((8, order), jnp.float32)

        @pl.when(is_left)
        def _():
            copies = []
            for i in range(3):
                to_ref, first = places[i]
                to_ref = to_ref.at[pl.ds(first, part), :]
                copies += unit_copies(root_ref, i + 1, rows, x, y, is_left, to_ref, sems, 2 * SIDE * i)
            finish(run(copies))

        @pl.when(jnp.logical_not(is_left))
        def _():
            copies = cross_copies(root_ref, 1, b_ref.at[pl.ds(0, part), :], sems, 0)
            for i in range(2):
                at = pl.ds(i * half, half)
                copies.append(pltpu.make_async_copy(root_ref.at[at, at], buf.at[i], sems.at[2 + i]))
            finish(run(copies))
            row = lax.broadcasted_iota(jnp.int32, (quarter, quarter), 0)
            col = lax.broadcasted_iota(jnp.int32, (quarter, quarter), 1)
            for i in range(2):
                low = buf[i, quarter:, quarter:]
                both = jnp.where(row <= col, buf[i, :quarter, :quarter], low)
                out_ref, first = places[i + 1]
                at = slice(first, first + part)
                for h in range(2):
                    out_ref[at, h * half : h * half + quarter] = buf[i, h * part : (h + 1) * part, quarter:]
                    out_ref[at, h * half + quarter : (h + 1) * half] = both[h * part : (h + 1) * part]
                out_ref[first + part : first + part + 1, :quarter] = jnp.sum(
                    jnp.where(row == col, low, 0.0), axis=0, keepdims=True
                )

    return call(
        body,
        [f32(2 * part + 8, order), f32(part + 8, order)],
        [HBM],
        [VMEM, VMEM],
        [pltpu.VMEM((2, half, half), jnp.float32), pltpu.SemaphoreType.DMA((6 * SIDE,))],
        0,
        24 * part * order,
    )(root)


def in_vmem(*shape, dtype=jnp.bfloat16):
    return pltpu.VMEM(shape, dtype)


def cut_two(src, high, low, tiles):
    def step(i, carry):
        at = pl.ds(pl.multiple_of(i * 64, 64), 64)
        high[at, :], low[at, :] = split(src[at, :])
        return carry

    lax.fori_loop(0, tiles, step, 0)


def split_root(root, rows):
    order = root.shape[0]

    def body(root_ref, high_ref, low_ref, buf, sems):
        x, y, is_left, outer = spot()

        @pl.when(is_left)
        def _():
            copies = []
            for k in range(2 * SIDE):
                row = rows_of(k, x, y, rows)
                copies.append(
                    pltpu.make_async_copy(
                        root_ref.at[pl.ds(pl.multiple_of(row, rows), rows), :],
                        buf.at[pl.ds(k * rows, rows), :],
                        sems.at[k],
                    )
                )
            finish(run(copies))
            cut_two(buf, high_ref, low_ref, order // 128)

        @pl.when(jnp.logical_not(is_left))
        def _():
            finish(run([pltpu.make_async_copy(root_ref, buf, sems.at[0])]))
            cut_two(buf, high_ref, low_ref, order // 64)

    return call(
        body,
        [in_vmem(order, order)] * 2,
        [HBM],
        [VMEM, VMEM],
        [pltpu.VMEM((order, order), jnp.float32), pltpu.SemaphoreType.DMA((2 * SIDE,))],
        0,
        8 * order * order,
    )(root)


def first_product(pieces, rows, r_high, r_low):
    order = r_high.shape[0]
    half, tile = order // 2, order // 4
    count = len(pieces)

    def body(*refs):
        piece_refs, (rh_ref, rl_ref) = refs[:count], refs[count : count + 2]
        gh_ref, gl_ref, high_ref, low_ref, buf, sems = refs[count + 2 :]
        x, y, is_left, outer = spot()
        from_y = (y, 3 - y, lax.bitwise_xor(y, 1), 3 - lax.bitwise_xor(y, 1))
        copies = []
        for k in range(count):
            row = (lax.bitwise_and(x - k % SIDE, 3) * SIDE + from_y[k // SIDE]) * rows
            copies.append(
                pltpu.make_async_copy(
                    piece_refs[k].at[pl.ds(pieces[k][1], rows), :],
                    buf.at[pl.ds(pl.multiple_of(row, rows), rows), :],
                    sems.at[k],
                )
            )
        finish(run(copies))
        cut_two(buf, gh_ref, gl_ref, order // 64)

        def product(a_high, a_low, b_high, b_low, tiles):
            def step(i, carry):
                at = pl.ds(pl.multiple_of(i * tile, tile), tile)
                for n in range(2):
                    cols = slice(n * half, (n + 1) * half)
                    acc = mul_split(a_high[at, :], a_low[at, :], b_high[:, cols], b_low[:, cols])
                    high_ref[at, cols], low_ref[at, cols] = split(acc)
                return carry

            lax.fori_loop(0, tiles, step, 0)

        @pl.when(is_left)
        def _():
            product(rh_ref, rl_ref, gh_ref, gl_ref, 2)

        @pl.when(jnp.logical_not(is_left))
        def _():
            product(gh_ref, gl_ref, rh_ref, rl_ref, 4)

    return call(
        body,
        [in_vmem(order, order)] * 4,
        [HBM] * count + [VMEM] * 2,
        [VMEM] * 4,
        [pltpu.VMEM((order, order), jnp.float32), pltpu.SemaphoreType.DMA((count,))],
        0,
        order * order,
    )(*(piece for piece, _ in pieces), r_high, r_low)


def unfold(c_ref, first, b_high, b_low, base):
    half = c_ref.shape[1] // 2
    quarter = half // 2
    mid = quarter // 2
    row = lax.broadcasted_iota(jnp.int32, (quarter, quarter), 0)
    col = lax.broadcasted_iota(jnp.int32, (quarter, quarter), 1)
    at = slice(first, first + mid)
    cross = jnp.concatenate([c_ref[at, :quarter], c_ref[at, half : half + quarter]], axis=0)
    both = jnp.concatenate([c_ref[at, quarter:half], c_ref[at, half + quarter :]], axis=0)
    diag = c_ref[first + mid : first + mid + 1, :quarter]
    turned = both.T
    top = jnp.where(row <= col, both, turned)
    low = jnp.where(row > col, both, jnp.where(row == col, diag, turned))
    for r, left_mat, right_mat in ((0, top, cross), (1, cross.T, low)):
        at = slice(base + r * quarter, base + (r + 1) * quarter)
        b_high[at, :quarter], b_low[at, :quarter] = split(left_mat)
        b_high[at, quarter:], b_low[at, quarter:] = split(right_mat)


def second_product(which, t_high, t_low, chunks, squares):
    order = t_high.shape[0]
    half, quarter, eighth = order // 2, order // 4, order // 8
    dests = 2 * SIDE
    part = quarter // dests
    few = part // 2
    count = len(chunks)

    def body(*refs):
        sources, sq_ref = refs[: 2 + count], refs[2 + count]
        whole, sq_out, b_high, b_low, *buffers = refs[3 + count :]
        sems = buffers.pop()
        x, y, is_left, outer = spot()
        finish(
            run(
                [
                    pltpu.make_async_copy(source, buffer, sems.at[i])
                    for i, (source, buffer) in enumerate(zip(sources, buffers))
                ]
            )
        )
        high_ref, low_ref, *chunk_refs = buffers
        outs = []
        for k in range(dests):
            to_y = 3 - y if k % 2 else y
            outs.append(whole.at[2 * lax.bitwise_and(x + k // 2, 3) + lax.shift_right_logical(to_y, 1)])
        units = [(chunk_refs[0], 0), (chunk_refs[1], 0), (chunk_refs[1], eighth), (chunk_refs[-1], 0)]

        @pl.when(is_left)
        def _():
            for q in range(4):
                c_ref, first = units[q // 2]
                at = slice(q * eighth, (q + 1) * eighth)
                mat = c_ref[first : first + eighth, (q % 2) * half : (q % 2 + 1) * half]
                if which == 0:
                    b_high[half:, at], b_low[half:, at] = split(mat.T)
                else:
                    b_high[at, :], b_low[at, :] = split(mat)
            unfold(*units[2 + which], b_high, b_low, half * which)
            total = jnp.float32(0.0)
            for m in range(2):
                at = slice(m * quarter, (m + 1) * quarter)
                acc = mul_split(high_ref[at, :], low_ref[at, :], b_high[...], b_low[...])
                total = total + jnp.sum(acc * acc)
                for k in range(SIDE):
                    for h in range(2):
                        first = (2 * k + h) * part
                        for q in range(SIDE):
                            at = slice((h * SIDE + q) * part, (h * SIDE + q + 1) * part)
                            lanes = slice(q * 128, (q + 1) * 128)
                            outs[m * SIDE + k][at, :] = acc[first : first + part, lanes]
            sq_out[...] = sq_ref[...] + total

        @pl.when(jnp.logical_not(is_left))
        def _():
            mats = []
            for c_ref, first in units[2 * which : 2 * which + 2]:
                mats.append(c_ref[first : first + eighth, :])
            a_high, a_low = split(jnp.concatenate(mats, axis=0))
            total = jnp.float32(0.0)
            for n in range(2):
                cols = slice(n * half, (n + 1) * half)
                acc = mul_split(a_high, a_low, high_ref[:, cols], low_ref[:, cols])
                total = total + jnp.sum(acc * acc)
                for k in range(dests):
                    for q in range(SIDE):
                        first = (n * SIDE + q) * part
                        lanes = slice(q * 128, (q + 1) * 128)
                        outs[k][first : first + few, :] = acc[k * few : (k + 1) * few, lanes]
                        outs[k][first + few : first + part, :] = acc[
                            eighth + k * few : eighth + (k + 1) * few, lanes
                        ]
            sq_out[...] = sq_ref[...] + total

    short = pltpu.VMEM((order, half), jnp.bfloat16)
    return call(
        body,
        [pltpu.HBM((dests, 8 * part + 8 * which, 128), jnp.float32), f32(8, 128)],
        [HBM] * (2 + count) + [VMEM],
        [VMEM] * 2,
        [short, short]
        + [pltpu.VMEM(v.shape, v.dtype) for v in (t_high, t_low, *chunks)]
        + [pltpu.SemaphoreType.DMA((2 + count,))],
        0,
        0,
    )(t_high, t_low, *chunks, squares)


def update_statistics(g_high, g_low, stat):
    order = g_high.shape[0]
    tile = order // 4
    tiles = order // tile

    def body(gh_ref, gl_ref, s_ref, out_ref, zero_ref, high, low):
        x, y, is_left, outer = spot()
        zero_ref[...] = jnp.zeros((8, 128), jnp.float32)

        @pl.when(is_left)
        def _():
            high[...] = gh_ref[...]
            low[...] = gl_ref[...]

        @pl.when(jnp.logical_not(is_left))
        def _():
            for i in range(tiles):
                for j in range(tiles):
                    at, cols = slice(i * tile, (i + 1) * tile), slice(j * tile, (j + 1) * tile)
                    high[at, cols] = gh_ref[cols, at].T
                    low[at, cols] = gl_ref[cols, at].T

        def outer_mul(a, b):
            return lax.dot_general(a, b, (((1,), (1,)), ((), ())), preferred_element_type=jnp.float32)

        for i in range(tiles):
            at = slice(i * tile, (i + 1) * tile)
            for j in range(i, tiles):
                to = slice(j * tile, (j + 1) * tile)
                acc = outer_mul(high[at, :], high[to, :]) + (
                    outer_mul(high[at, :], low[to, :]) + outer_mul(low[at, :], high[to, :])
                )
                acc = (1.0 - BETA_STAT) * acc
                out_ref[at, to] = BETA_STAT * s_ref[at, to] + acc
                if i != j:
                    out_ref[to, at] = BETA_STAT * s_ref[to, at] + acc.T

    short = pltpu.VMEM((order, order), jnp.bfloat16)
    return call(
        body,
        [f32(order, order), f32(8, 128)],
        [VMEM, VMEM, VMEM],
        [VMEM, VMEM],
        [short, short],
        0,
        order * order,
        24,
    )(g_high, g_low, stat)


def place_columns(first, second, sums, totals, owner_table, largest):
    count = first.shape[0]
    part = first.shape[1] // 8
    order = 8 * first.shape[2]
    end = 8 * part

    def body(owner_ref, first_ref, second_ref, sums_ref, totals_ref, out_ref, scratch):
        x, y, is_left, outer = spot()
        total = jnp.sum(jnp.sum(totals_ref[...], axis=0, keepdims=True), axis=1, keepdims=True)
        clip = jnp.minimum(1.0, largest / jnp.sqrt(total + 1e-06))
        scratch[...] = jnp.broadcast_to(jnp.sum(sums_ref[...], axis=1, keepdims=True), (count, 128))
        for c in range(count):
            p = owner_ref[0, c]
            from_left = (lax.bitwise_and(p, 1) == 0) == outer
            squares = second_ref[p, end : end + 1, :]
            scale = jnp.sqrt(scratch[c : c + 1, :] / (squares + 1e-06)) * clip
            for j in range(8):
                cols = slice(c * order + j * 128, c * order + (j + 1) * 128)
                at = slice(j * part, (j + 1) * part)
                back = (j + 4) % 8
                across = slice(back * part, (back + 1) * part)
                if j < 4:
                    out_ref[:part, cols] = first_ref[p, at, :] * scale
                    other = jnp.where(from_left, first_ref[p, across, :], second_ref[p, at, :])
                    out_ref[part:, cols] = other * scale
                else:
                    other = jnp.where(from_left, second_ref[p, across, :], first_ref[p, at, :])
                    out_ref[:part, cols] = other * scale
                    out_ref[part:, cols] = second_ref[p, at, :] * scale

    return call(
        body,
        f32(2 * part, count * order),
        [SMEM] + [VMEM] * 4,
        VMEM,
        [pltpu.VMEM((count, 128), jnp.float32)],
        0,
        16 * count * part * order,
    )(owner_table, first, second, sums, totals)


def with_squares(parts, squares):
    rows = parts.shape[1]

    def body(parts_ref, squares_ref, out_ref):
        for k in range(parts.shape[0]):
            out_ref[k] = squares_ref[...]

    return pl.pallas_call(
        body,
        grid=(1,),
        out_shape=f32(*parts.shape),
        in_specs=[pl.BlockSpec(memory_space=pl.ANY), pl.BlockSpec((8, 128), lambda i: (0, 0))],
        out_specs=pl.BlockSpec((parts.shape[0], 8, 128), lambda i: (0, rows // 8 - 1, 0)),
        input_output_aliases={0: 0},
    )(parts, squares)


def sent_back(parts):
    return lax.all_to_all(parts, "dp", 0, 0, axis_index_groups=GROUPS, tiled=True)


def local(gradient, moment, second, statistics, inv_roots, owner_table):
    rows_dev, width = gradient.shape
    order = statistics.shape[1]
    col_blocks = width // order
    root = inv_roots[0]

    lead, oth, x1, x2, x3 = cut(gradient, root, owner_table)
    lead_got = near(lead)
    far_y = {0: far(oth)}
    new_moment, new_second, own_sums = adam(gradient, moment, second, order)
    got_x = {1: along_x(x1, 1), 3: along_x(x3, 3)}
    got_x[2] = along_x(tie(x2, far_y[0], got_x[1], got_x[3], own_sums), 2)
    own_y = {d: got_x[d][:rows_dev] for d in (1, 2, 3)}
    oth_y = {d: got_x[d][rows_dev:] for d in (1, 2, 3)}
    for d in (1, 2, 3):
        far_y[d] = far(oth_y[d])

    chunk_b, chunk_c = pack(root, rows_dev)
    r_high, r_low = split_root(root, rows_dev)
    near_own = {1: near(tie(own_y[1], lead_got))}
    near_far = {0: near(tie(far_y[0], lead_got))}
    near_own[3] = near(tie(own_y[3], near_own[1], far_y[1], far_y[3]))
    near_far[1] = near(tie(far_y[1], near_far[0], got_x[2]))
    near_far[3] = near(tie(far_y[3], near_own[3]))
    near_own[2] = near(tie(own_y[2], near_far[1], far_y[2], chunk_b, chunk_c, r_high))
    near_far[2] = near(tie(far_y[2], near_far[3]))

    chunk_b = near(tie(chunk_b, near_own[2], near_far[2]))
    chunk_c = near(tie(chunk_c, near_own[2], near_far[2]))

    lead_rows = lead.shape[0] - rows_dev
    pieces = [(lead, lead_rows)] + [(got_x[d], 0) for d in (1, 2, 3)]
    pieces += [(far_y[d], 0) for d in range(SIDE)]
    pieces += [(lead_got, lead_rows)] + [(near_own[d], 0) for d in (1, 2, 3)]
    pieces += [(near_far[d], 0) for d in range(SIDE)]
    g_high, g_low, t_high, t_low = first_product(pieces, rows_dev, r_high, r_low)
    new_stat, squares = update_statistics(g_high, g_low, statistics[0])
    sums = tie(own_sums, squares)
    for bit in (4, 8):
        sums = sums + swap(sums, "dp", bit)
    squares = tie(squares, sums)
    half_a, squares = second_product(0, t_high, t_low, [lead_got, chunk_b], squares)
    sums = tie(sums, squares)
    sums = sums + swap(sums, "dp", 3)
    back_a = sent_back(tie(half_a, chunk_c, sums))
    half_b, squares = second_product(1, t_high, t_low, [lead_got, chunk_b, chunk_c], squares)
    squares = squares + near(squares)
    totals = sums + swap(sums, "fsdp", 1)
    back_b = sent_back(tie(with_squares(half_b, tie(squares, totals)), back_a))
    totals = tie(totals, back_a)
    bit = 2
    while bit < lax.axis_size("fsdp"):
        totals = totals + swap(totals, "fsdp", bit)
        bit *= 2
    both = jnp.concatenate([sums, totals], axis=0)
    both = both + near(both)
    sums, totals = both[:col_blocks], both[col_blocks:]

    count_all = order * lax.axis_size("fsdp") * width
    update = place_columns(
        back_a, back_b, sums, totals, owner_table, CLIP_RMS * math.sqrt(count_all)
    )
    return (update, new_moment, new_second, new_stat[None])


def solution(mesh):
    placed = (
        P(("fsdp", "dp"), None),
        P(("fsdp", "dp"), None),
        P(("fsdp", "dp"), None),
        P(("fsdp", "dp"), None, None),
        P(("fsdp", "dp"), None, None),
        P("fsdp", None),
    )
    return jax.shard_map(
        local,
        mesh=mesh,
        in_specs=placed,
        out_specs=(
            P(("fsdp", "dp"), None),
            P(("fsdp", "dp"), None),
            P(("fsdp", "dp"), None),
            P(("fsdp", "dp"), None, None),
        ),
        check_vma=False,
    )
```

```python
import math

import jax
import jax.numpy as jnp
from jax import lax
from jax.experimental import pallas as pl
from jax.experimental.pallas import tpu as pltpu
from jax.sharding import PartitionSpec as P

BETA_STAT = 0.95
BETA_ONE = 0.9
BETA_TWO = 0.999
BIAS_ONE = 1.0 - 0.9**10
BIAS_TWO = 1.0 - 0.999**10
ADAM_EPS = 1e-08
CLIP_RMS = 0.25
SIDE = 4


def route(move):
    pairs = []
    for src in range(SIDE * SIDE):
        x, y = move(src // SIDE, src % SIDE)
        pairs.append((src, (x % SIDE) * SIDE + y % SIDE))
    return pairs


NEAR = route(lambda x, y: (x, y ^ 1))
FAR = route(lambda x, y: (x, 3 - y))
GROUPS = [
    [SIDE * x + y for x in range(SIDE) for y in (0, 3)],
    [SIDE * x + y for x in range(SIDE) for y in (1, 2)],
]


def near(v):
    return lax.ppermute(v, "dp", NEAR)


def far(v):
    return lax.ppermute(v, "dp", FAR)


def along_x(v, shift):
    return lax.ppermute(v, "dp", route(lambda x, y: (x + shift, y)))


def tie(v, *after):
    return lax.optimization_barrier((v, *after))[0]


def swap(v, axis, bit):
    count = lax.axis_size(axis)
    return lax.ppermute(v, axis, [(i, i ^ bit) for i in range(count)])

HBM = pl.BlockSpec(memory_space=pltpu.HBM)
VMEM = pl.BlockSpec(memory_space=pltpu.VMEM)
SMEM = pl.BlockSpec(memory_space=pltpu.SMEM)


def call(body, out, in_specs, out_specs, scratch, flops, moved, vmem=16):
    return pl.pallas_call(
        body,
        out_shape=out,
        in_specs=in_specs,
        out_specs=out_specs,
        scratch_shapes=scratch,
        compiler_params=pltpu.CompilerParams(vmem_limit_bytes=vmem * 2**20),
        cost_estimate=pl.CostEstimate(flops=flops, bytes_accessed=moved, transcendentals=0),
    )


def f32(*shape):
    return jax.ShapeDtypeStruct(shape, jnp.float32)


def spot():
    place = lax.axis_index("dp")
    x, y = lax.shift_right_logical(place, 2), lax.bitwise_and(place, 3)
    is_left = lax.bitwise_and(y, 1) == 0
    outer = jnp.logical_or(y == 0, y == 3)
    return x, y, is_left, outer


def rows_of(k, x, y, rows):
    return (lax.bitwise_and(x + k // 2, 3) * SIDE + (3 - y if k % 2 else y)) * rows


def run(copies):
    for copy in copies:
        copy.start()
    return copies


def finish(copies):
    for copy in copies:
        copy.wait()


def split(v):
    high = v.astype(jnp.bfloat16)
    return high, (v - high.astype(jnp.float32)).astype(jnp.bfloat16)


def mul(a, b):
    return jnp.dot(a, b, preferred_element_type=jnp.float32)


def mul_split(a_high, a_low, b_high, b_low):
    return mul(a_high, b_high) + (mul(a_high, b_low) + mul(a_low, b_high))


def unit_copies(root_ref, unit, rows, x, y, is_left, to_ref, sems, base):
    few = rows // 4
    copies = []
    for k in range(2 * SIDE):
        row = rows_of(k, x, lax.bitwise_xor(y, 1), rows) + unit * few
        copies.append(
            pltpu.make_async_copy(
                root_ref.at[pl.ds(pl.multiple_of(row, few), few), :],
                to_ref.at[pl.ds(k * few, few), :],
                sems.at[base + k],
            )
        )
    return copies


def cross_copies(root_ref, unit, to_ref, sems, base):
    order = root_ref.shape[0]
    half, part = order // 2, order // 8
    return [
        pltpu.make_async_copy(
            root_ref.at[pl.ds((2 * unit + h) * part, part), pl.ds(half, half)],
            to_ref.at[:, pl.ds(h * half, half)],
            sems.at[base + h],
        )
        for h in range(2)
    ]


def column_of(owner_ref, pos, count):
    col = jnp.int32(0)
    for c in range(count):
        col = col + jnp.where(owner_ref[0, c] == pos, c, 0)
    return col


def position(x, y, d, j):
    return 2 * lax.bitwise_and(x + d, 3) + lax.bitwise_xor(lax.shift_right_logical(y, 1), j)


def cut(gradient, root, owner_table):
    rows, width = gradient.shape
    order = root.shape[0]
    count = width // order
    part = order // 8
    sizes = [(part + rows, order), (rows, order)] + [(2 * rows, order)] * 3

    def body(owner_ref, g_ref, root_ref, lead_ref, oth_ref, x1_ref, x2_ref, x3_ref, sems):
        x, y, is_left, outer = spot()
        outs = [(lead_ref.at[pl.ds(part, rows), :], oth_ref)]
        outs += [(r.at[pl.ds(0, rows), :], r.at[pl.ds(rows, rows), :]) for r in (x1_ref, x2_ref, x3_ref)]
        copies = []
        for d in range(SIDE):
            for j in range(2):
                col = column_of(owner_ref, position(x, y, d, j), count)
                at = pl.ds(pl.multiple_of(col * order, order), order)
                copies.append(pltpu.make_async_copy(g_ref.at[:, at], outs[d][j], sems.at[2 * d + j]))
        run(copies)
        chunk_ref = lead_ref.at[pl.ds(0, part), :]

        @pl.when(is_left)
        def _():
            finish(run(unit_copies(root_ref, 0, rows, x, y, is_left, chunk_ref, sems, 2 * SIDE)))

        @pl.when(jnp.logical_not(is_left))
        def _():
            finish(run(cross_copies(root_ref, 0, chunk_ref, sems, 2 * SIDE)))

        finish(copies)

    return call(
        body,
        [in_vmem(*size, dtype=jnp.float32) for size in sizes],
        [SMEM, HBM, HBM],
        [VMEM] * 5,
        [pltpu.SemaphoreType.DMA((4 * SIDE,))],
        0,
        8 * rows * width,
        60,
    )(owner_table, gradient, root)


def adam(gradient, moment, second, order):
    rows, width = gradient.shape
    count = width // order

    def body(g_ref, m_ref, s_ref, m_out, s_out, sums_ref):
        def step(i, total):
            at = pl.ds(pl.multiple_of(i * 8, 8), 8)
            g = g_ref[at, :]
            new_m = BETA_ONE * m_ref[at, :] + (1.0 - BETA_ONE) * g
            new_s = BETA_TWO * s_ref[at, :] + (1.0 - BETA_TWO) * g * g
            m_out[at, :] = new_m
            s_out[at, :] = new_s
            a = new_m / BIAS_ONE / (jnp.sqrt(new_s / BIAS_TWO) + ADAM_EPS)
            return total + a * a

        total = lax.fori_loop(0, rows // 8, step, jnp.zeros((8, 2 * order), jnp.float32))
        total = jnp.sum(total, axis=0, keepdims=True)
        for h in range(2):
            sums_ref[pl.ds(2 * pl.program_id(0) + h, 1), :] = total[:, h * order : (h + 1) * order]

    block = pl.BlockSpec((rows, 2 * order), lambda c: (0, c))
    return pl.pallas_call(
        body,
        grid=(count // 2,),
        out_shape=[f32(rows, width)] * 2 + [f32(8, order)],
        in_specs=[block] * 3,
        out_specs=[block] * 2 + [pl.BlockSpec((8, order), lambda c: (0, 0))],
        compiler_params=pltpu.CompilerParams(vmem_limit_bytes=40 * 2**20),
        cost_estimate=pl.CostEstimate(flops=0, bytes_accessed=24 * rows * width, transcendentals=0),
    )(gradient, moment, second)


def pack(root, rows):
    order = root.shape[0]
    half, quarter, part = order // 2, order // 4, order // 8

    def body(root_ref, b_ref, c_ref, buf, sems):
        x, y, is_left, outer = spot()
        places = [(b_ref, 0), (b_ref, part), (c_ref, 0)]
        b_ref[2 * part :, :] = jnp.zeros((8, order), jnp.float32)

        @pl.when(is_left)
        def _():
            copies = []
            for i in range(3):
                to_ref, first = places[i]
                to_ref = to_ref.at[pl.ds(first, part), :]
                copies += unit_copies(root_ref, i + 1, rows, x, y, is_left, to_ref, sems, 2 * SIDE * i)
            finish(run(copies))

        @pl.when(jnp.logical_not(is_left))
        def _():
            copies = cross_copies(root_ref, 1, b_ref.at[pl.ds(0, part), :], sems, 0)
            for i in range(2):
                at = pl.ds(i * half, half)
                copies.append(pltpu.make_async_copy(root_ref.at[at, at], buf.at[i], sems.at[2 + i]))
            finish(run(copies))
            row = lax.broadcasted_iota(jnp.int32, (quarter, quarter), 0)
            col = lax.broadcasted_iota(jnp.int32, (quarter, quarter), 1)
            for i in range(2):
                low = buf[i, quarter:, quarter:]
                both = jnp.where(row <= col, buf[i, :quarter, :quarter], low)
                out_ref, first = places[i + 1]
                at = slice(first, first + part)
                for h in range(2):
                    out_ref[at, h * half : h * half + quarter] = buf[i, h * part : (h + 1) * part, quarter:]
                    out_ref[at, h * half + quarter : (h + 1) * half] = both[h * part : (h + 1) * part]
                b_ref[2 * part + i : 2 * part + i + 1, :quarter] = jnp.sum(
                    jnp.where(row == col, low, 0.0), axis=0, keepdims=True
                )

    return call(
        body,
        [f32(2 * part + 8, order), f32(part, order)],
        [HBM],
        [VMEM, VMEM],
        [pltpu.VMEM((2, half, half), jnp.float32), pltpu.SemaphoreType.DMA((6 * SIDE,))],
        0,
        24 * part * order,
    )(root)


def in_vmem(*shape, dtype=jnp.bfloat16):
    return pltpu.VMEM(shape, dtype)


def cut_two(src, high, low, tiles):
    def step(i, carry):
        at = pl.ds(pl.multiple_of(i * 64, 64), 64)
        high[at, :], low[at, :] = split(src[at, :])
        return carry

    lax.fori_loop(0, tiles, step, 0)


def split_root(root, rows):
    order = root.shape[0]

    def body(root_ref, high_ref, low_ref, buf, sems):
        x, y, is_left, outer = spot()

        @pl.when(is_left)
        def _():
            copies = []
            for k in range(2 * SIDE):
                row = rows_of(k, x, y, rows)
                copies.append(
                    pltpu.make_async_copy(
                        root_ref.at[pl.ds(pl.multiple_of(row, rows), rows), :],
                        buf.at[pl.ds(k * rows, rows), :],
                        sems.at[k],
                    )
                )
            finish(run(copies))
            cut_two(buf, high_ref, low_ref, order // 128)

        @pl.when(jnp.logical_not(is_left))
        def _():
            finish(run([pltpu.make_async_copy(root_ref, buf, sems.at[0])]))
            cut_two(buf, high_ref, low_ref, order // 64)

    return call(
        body,
        [in_vmem(order, order)] * 2,
        [HBM],
        [VMEM, VMEM],
        [pltpu.VMEM((order, order), jnp.float32), pltpu.SemaphoreType.DMA((2 * SIDE,))],
        0,
        8 * order * order,
    )(root)


def first_product(pieces, rows, r_high, r_low):
    order = r_high.shape[0]
    half, tile = order // 2, order // 4
    count = len(pieces)

    def body(*refs):
        piece_refs, (rh_ref, rl_ref) = refs[:count], refs[count : count + 2]
        gh_ref, gl_ref, high_ref, low_ref, buf, sems = refs[count + 2 :]
        x, y, is_left, outer = spot()
        from_y = (y, 3 - y, lax.bitwise_xor(y, 1), 3 - lax.bitwise_xor(y, 1))
        copies = []
        for k in range(count):
            row = (lax.bitwise_and(x - k % SIDE, 3) * SIDE + from_y[k // SIDE]) * rows
            copies.append(
                pltpu.make_async_copy(
                    piece_refs[k].at[pl.ds(pieces[k][1], rows), :],
                    buf.at[pl.ds(pl.multiple_of(row, rows), rows), :],
                    sems.at[k],
                )
            )
        finish(run(copies))
        cut_two(buf, gh_ref, gl_ref, order // 64)

        def product(a_high, a_low, b_high, b_low, tiles):
            def step(i, carry):
                at = pl.ds(pl.multiple_of(i * tile, tile), tile)
                for n in range(2):
                    cols = slice(n * half, (n + 1) * half)
                    acc = mul_split(a_high[at, :], a_low[at, :], b_high[:, cols], b_low[:, cols])
                    high_ref[at, cols], low_ref[at, cols] = split(acc)
                return carry

            lax.fori_loop(0, tiles, step, 0)

        @pl.when(is_left)
        def _():
            product(rh_ref, rl_ref, gh_ref, gl_ref, 2)

        @pl.when(jnp.logical_not(is_left))
        def _():
            product(gh_ref, gl_ref, rh_ref, rl_ref, 4)

    return call(
        body,
        [in_vmem(order, order)] * 4,
        [HBM] * count + [VMEM] * 2,
        [VMEM] * 4,
        [pltpu.VMEM((order, order), jnp.float32), pltpu.SemaphoreType.DMA((count,))],
        0,
        order * order,
    )(*(piece for piece, _ in pieces), r_high, r_low)


def unfold(c_ref, first, diag, b_high, b_low, base):
    half = c_ref.shape[1] // 2
    quarter = half // 2
    mid = quarter // 2
    row = lax.broadcasted_iota(jnp.int32, (quarter, quarter), 0)
    col = lax.broadcasted_iota(jnp.int32, (quarter, quarter), 1)
    at = slice(first, first + mid)
    cross = jnp.concatenate([c_ref[at, :quarter], c_ref[at, half : half + quarter]], axis=0)
    both = jnp.concatenate([c_ref[at, quarter:half], c_ref[at, half + quarter :]], axis=0)
    turned = both.T
    top = jnp.where(row <= col, both, turned)
    low = jnp.where(row > col, both, jnp.where(row == col, diag, turned))
    for r, left_mat, right_mat in ((0, top, cross), (1, cross.T, low)):
        at = slice(base + r * quarter, base + (r + 1) * quarter)
        b_high[at, :quarter], b_low[at, :quarter] = split(left_mat)
        b_high[at, quarter:], b_low[at, quarter:] = split(right_mat)


def second_product(which, t_high, t_low, chunks, squares):
    order = t_high.shape[0]
    half, quarter, eighth = order // 2, order // 4, order // 8
    dests = 2 * SIDE
    part = quarter // dests
    few = part // 2
    count = len(chunks)

    def body(high_ref, low_ref, *refs):
        chunk_refs, sq_ref = refs[:count], refs[count]
        whole, sq_out, b_high, b_low = refs[count + 1 :]
        x, y, is_left, outer = spot()
        outs = []
        for k in range(dests):
            to_y = 3 - y if k % 2 else y
            outs.append(whole.at[2 * lax.bitwise_and(x + k // 2, 3) + lax.shift_right_logical(to_y, 1)])
        units = [(chunk_refs[0], 0), (chunk_refs[1], 0), (chunk_refs[1], eighth), (chunk_refs[-1], 0)]

        @pl.when(is_left)
        def _():
            for q in range(4):
                c_ref, first = units[q // 2]
                at = slice(q * eighth, (q + 1) * eighth)
                mat = c_ref[first : first + eighth, (q % 2) * half : (q % 2 + 1) * half]
                if which == 0:
                    b_high[half:, at], b_low[half:, at] = split(mat.T)
                else:
                    b_high[at, :], b_low[at, :] = split(mat)
            row = 2 * eighth + which
            diag = chunk_refs[1][row : row + 1, :quarter]
            unfold(*units[2 + which], diag, b_high, b_low, half * which)
            total = jnp.float32(0.0)
            for m in range(2):
                at = slice(m * quarter, (m + 1) * quarter)
                acc = mul_split(high_ref[at, :], low_ref[at, :], b_high[...], b_low[...])
                total = total + jnp.sum(acc * acc)
                for k in range(SIDE):
                    for h in range(2):
                        first = (2 * k + h) * part
                        for q in range(SIDE):
                            at = slice((h * SIDE + q) * part, (h * SIDE + q + 1) * part)
                            lanes = slice(q * 128, (q + 1) * 128)
                            outs[m * SIDE + k][at, :] = acc[first : first + part, lanes]
            sq_out[...] = sq_ref[...] + total

        @pl.when(jnp.logical_not(is_left))
        def _():
            mats = []
            for c_ref, first in units[2 * which : 2 * which + 2]:
                mats.append(c_ref[first : first + eighth, :])
            a_high, a_low = split(jnp.concatenate(mats, axis=0))
            total = jnp.float32(0.0)
            for n in range(2):
                cols = slice(n * half, (n + 1) * half)
                acc = mul_split(a_high, a_low, high_ref[:, cols], low_ref[:, cols])
                total = total + jnp.sum(acc * acc)
                for k in range(dests):
                    for q in range(SIDE):
                        first = (n * SIDE + q) * part
                        lanes = slice(q * 128, (q + 1) * 128)
                        outs[k][first : first + few, :] = acc[k * few : (k + 1) * few, lanes]
                        outs[k][first + few : first + part, :] = acc[
                            eighth + k * few : eighth + (k + 1) * few, lanes
                        ]
            sq_out[...] = sq_ref[...] + total

    short = pltpu.VMEM((order, half), jnp.bfloat16)
    return call(
        body,
        [pltpu.HBM((dests, 8 * part + 8 * which, 128), jnp.float32), f32(8, 128)],
        [VMEM] * (3 + count),
        [VMEM] * 2,
        [short, short],
        0,
        0,
        8,
    )(t_high, t_low, *chunks, squares)


def update_statistics(g_high, g_low, stat):
    order = g_high.shape[0]
    tile = order // 4
    tiles = order // tile

    def body(gh_ref, gl_ref, s_ref, out_ref, zero_ref, high, low):
        x, y, is_left, outer = spot()
        zero_ref[...] = jnp.zeros((8, 128), jnp.float32)

        @pl.when(is_left)
        def _():
            high[...] = gh_ref[...]
            low[...] = gl_ref[...]

        @pl.when(jnp.logical_not(is_left))
        def _():
            for i in range(tiles):
                for j in range(tiles):
                    at, cols = slice(i * tile, (i + 1) * tile), slice(j * tile, (j + 1) * tile)
                    high[at, cols] = gh_ref[cols, at].T
                    low[at, cols] = gl_ref[cols, at].T

        def outer_mul(a, b):
            return lax.dot_general(a, b, (((1,), (1,)), ((), ())), preferred_element_type=jnp.float32)

        for i in range(tiles):
            at = slice(i * tile, (i + 1) * tile)
            for j in range(i, tiles):
                to = slice(j * tile, (j + 1) * tile)
                acc = outer_mul(high[at, :], high[to, :]) + (
                    outer_mul(high[at, :], low[to, :]) + outer_mul(low[at, :], high[to, :])
                )
                acc = (1.0 - BETA_STAT) * acc
                out_ref[at, to] = BETA_STAT * s_ref[at, to] + acc
                if i != j:
                    out_ref[to, at] = BETA_STAT * s_ref[to, at] + acc.T

    short = pltpu.VMEM((order, order), jnp.bfloat16)
    return call(
        body,
        [f32(order, order), f32(8, 128)],
        [VMEM, VMEM, VMEM],
        [VMEM, VMEM],
        [short, short],
        0,
        order * order,
        14,
    )(g_high, g_low, stat)


def place_columns(first, second, sums, totals, owner_table, largest):
    count = first.shape[0]
    part = first.shape[1] // 8
    order = 8 * first.shape[2]
    end = 8 * part

    def body(owner_ref, first_ref, second_ref, sums_ref, totals_ref, out_ref, scratch):
        x, y, is_left, outer = spot()
        total = jnp.sum(jnp.sum(totals_ref[...], axis=0, keepdims=True), axis=1, keepdims=True)
        clip = jnp.minimum(1.0, largest / jnp.sqrt(total + 1e-06))
        scratch[...] = jnp.broadcast_to(jnp.sum(sums_ref[...], axis=1, keepdims=True), (count, 128))
        for c in range(count):
            p = owner_ref[0, c]
            from_left = (lax.bitwise_and(p, 1) == 0) == outer
            squares = second_ref[p, end : end + 1, :]
            scale = jnp.sqrt(scratch[c : c + 1, :] / (squares + 1e-06)) * clip
            for j in range(8):
                cols = slice(c * order + j * 128, c * order + (j + 1) * 128)
                at = slice(j * part, (j + 1) * part)
                back = (j + 4) % 8
                across = slice(back * part, (back + 1) * part)
                if j < 4:
                    out_ref[:part, cols] = first_ref[p, at, :] * scale
                    other = jnp.where(from_left, first_ref[p, across, :], second_ref[p, at, :])
                    out_ref[part:, cols] = other * scale
                else:
                    other = jnp.where(from_left, second_ref[p, across, :], first_ref[p, at, :])
                    out_ref[:part, cols] = other * scale
                    out_ref[part:, cols] = second_ref[p, at, :] * scale

    return call(
        body,
        f32(2 * part, count * order),
        [SMEM] + [VMEM] * 4,
        VMEM,
        [pltpu.VMEM((count, 128), jnp.float32)],
        0,
        16 * count * part * order,
    )(owner_table, first, second, sums, totals)


def with_squares(parts, squares):
    rows = parts.shape[1]

    def body(parts_ref, squares_ref, out_ref):
        for k in range(parts.shape[0]):
            out_ref[k] = squares_ref[...]

    return pl.pallas_call(
        body,
        grid=(1,),
        out_shape=f32(*parts.shape),
        in_specs=[pl.BlockSpec(memory_space=pl.ANY), pl.BlockSpec((8, 128), lambda i: (0, 0))],
        out_specs=pl.BlockSpec((parts.shape[0], 8, 128), lambda i: (0, rows // 8 - 1, 0)),
        input_output_aliases={0: 0},
    )(parts, squares)


def sent_back(parts):
    return lax.all_to_all(parts, "dp", 0, 0, axis_index_groups=GROUPS, tiled=True)


def local(gradient, moment, second, statistics, inv_roots, owner_table):
    rows_dev, width = gradient.shape
    order = statistics.shape[1]
    col_blocks = width // order
    root = inv_roots[0]

    lead, oth, x1, x2, x3 = cut(gradient, root, owner_table)
    lead_got = near(lead)
    far_y = {0: far(oth)}
    new_moment, new_second, own_sums = adam(gradient, moment, second, order)
    got_x = {1: along_x(x1, 1), 3: along_x(x3, 3)}
    got_x[2] = along_x(tie(x2, far_y[0], got_x[1], got_x[3], own_sums), 2)
    own_y = {d: got_x[d][:rows_dev] for d in (1, 2, 3)}
    oth_y = {d: got_x[d][rows_dev:] for d in (1, 2, 3)}
    for d in (1, 2, 3):
        far_y[d] = far(oth_y[d])

    chunk_b, chunk_c = pack(root, rows_dev)
    r_high, r_low = split_root(root, rows_dev)
    near_own = {1: near(tie(own_y[1], lead_got))}
    near_far = {0: near(tie(far_y[0], lead_got))}
    near_own[3] = near(tie(own_y[3], near_own[1], far_y[1], far_y[3]))
    near_far[1] = near(tie(far_y[1], near_far[0], got_x[2]))
    near_far[3] = near(tie(far_y[3], near_own[3]))
    near_own[2] = near(tie(own_y[2], near_far[1], far_y[2], chunk_b, chunk_c, r_high))
    near_far[2] = near(tie(far_y[2], near_far[3]))

    chunk_b = near(tie(chunk_b, near_own[2], near_far[2]))
    chunk_c = near(tie(chunk_c, near_own[2], near_far[2]))

    lead_rows = lead.shape[0] - rows_dev
    pieces = [(lead, lead_rows)] + [(got_x[d], 0) for d in (1, 2, 3)]
    pieces += [(far_y[d], 0) for d in range(SIDE)]
    pieces += [(lead_got, lead_rows)] + [(near_own[d], 0) for d in (1, 2, 3)]
    pieces += [(near_far[d], 0) for d in range(SIDE)]
    g_high, g_low, t_high, t_low = first_product(pieces, rows_dev, r_high, r_low)
    new_stat, squares = update_statistics(g_high, g_low, statistics[0])
    sums = tie(own_sums, squares)
    for bit in (4, 8):
        sums = sums + swap(sums, "dp", bit)
    squares = tie(squares, sums)
    half_a, squares = second_product(0, t_high, t_low, [lead_got, chunk_b], squares)
    sums = tie(sums, squares)
    sums = sums + swap(sums, "dp", 3)
    back_a = sent_back(tie(half_a, chunk_c, sums))
    half_b, squares = second_product(1, t_high, t_low, [lead_got, chunk_b, chunk_c], squares)
    squares = squares + near(squares)
    totals = sums + swap(sums, "fsdp", 1)
    back_b = sent_back(tie(with_squares(half_b, tie(squares, totals)), back_a))
    totals = tie(totals, back_a)
    bit = 2
    while bit < lax.axis_size("fsdp"):
        totals = totals + swap(totals, "fsdp", bit)
        bit *= 2
    both = jnp.concatenate([sums, totals], axis=0)
    both = both + near(both)
    sums, totals = both[:col_blocks], both[col_blocks:]

    count_all = order * lax.axis_size("fsdp") * width
    update = place_columns(
        back_a, back_b, sums, totals, owner_table, CLIP_RMS * math.sqrt(count_all)
    )
    return (update, new_moment, new_second, new_stat[None])


def solution(mesh):
    placed = (
        P(("fsdp", "dp"), None),
        P(("fsdp", "dp"), None),
        P(("fsdp", "dp"), None),
        P(("fsdp", "dp"), None, None),
        P(("fsdp", "dp"), None, None),
        P("fsdp", None),
    )
    return jax.shard_map(
        local,
        mesh=mesh,
        in_specs=placed,
        out_specs=(
            P(("fsdp", "dp"), None),
            P(("fsdp", "dp"), None),
            P(("fsdp", "dp"), None),
            P(("fsdp", "dp"), None, None),
        ),
        check_vma=False,
    )
```

```python
import math

import jax
import jax.numpy as jnp
from jax import lax
from jax.experimental import pallas as pl
from jax.experimental.pallas import tpu as pltpu
from jax.sharding import PartitionSpec as P

BETA_STAT = 0.95
BETA_ONE = 0.9
BETA_TWO = 0.999
BIAS_ONE = 1.0 - 0.9**10
BIAS_TWO = 1.0 - 0.999**10
ADAM_EPS = 1e-08
CLIP_RMS = 0.25
SIDE = 4


def route(move):
    pairs = []
    for src in range(SIDE * SIDE):
        x, y = move(src // SIDE, src % SIDE)
        pairs.append((src, (x % SIDE) * SIDE + y % SIDE))
    return pairs


NEAR = route(lambda x, y: (x, y ^ 1))
FAR = route(lambda x, y: (x, 3 - y))
GROUPS = [
    [SIDE * x + y for x in range(SIDE) for y in (0, 3)],
    [SIDE * x + y for x in range(SIDE) for y in (1, 2)],
]


def near(v):
    return lax.ppermute(v, "dp", NEAR)


def far(v):
    return lax.ppermute(v, "dp", FAR)


def along_x(v, shift):
    return lax.ppermute(v, "dp", route(lambda x, y: (x + shift, y)))


def tie(v, *after):
    return lax.optimization_barrier((v, *after))[0]


def swap(v, axis, bit):
    count = lax.axis_size(axis)
    return lax.ppermute(v, axis, [(i, i ^ bit) for i in range(count)])

HBM = pl.BlockSpec(memory_space=pltpu.HBM)
VMEM = pl.BlockSpec(memory_space=pltpu.VMEM)
SMEM = pl.BlockSpec(memory_space=pltpu.SMEM)


def call(body, out, in_specs, out_specs, scratch, flops, moved, vmem=16):
    return pl.pallas_call(
        body,
        out_shape=out,
        in_specs=in_specs,
        out_specs=out_specs,
        scratch_shapes=scratch,
        compiler_params=pltpu.CompilerParams(vmem_limit_bytes=vmem * 2**20),
        cost_estimate=pl.CostEstimate(flops=flops, bytes_accessed=moved, transcendentals=0),
    )


def f32(*shape):
    return jax.ShapeDtypeStruct(shape, jnp.float32)


def spot():
    place = lax.axis_index("dp")
    x, y = lax.shift_right_logical(place, 2), lax.bitwise_and(place, 3)
    is_left = lax.bitwise_and(y, 1) == 0
    outer = jnp.logical_or(y == 0, y == 3)
    return x, y, is_left, outer


def rows_of(k, x, y, rows):
    return (lax.bitwise_and(x + k // 2, 3) * SIDE + (3 - y if k % 2 else y)) * rows


def run(copies):
    for copy in copies:
        copy.start()
    return copies


def finish(copies):
    for copy in copies:
        copy.wait()


def split(v):
    high = v.astype(jnp.bfloat16)
    return high, (v - high.astype(jnp.float32)).astype(jnp.bfloat16)


def mul(a, b):
    return jnp.dot(a, b, preferred_element_type=jnp.float32)


def mul_split(a_high, a_low, b_high, b_low):
    return mul(a_high, b_high) + (mul(a_high, b_low) + mul(a_low, b_high))


def unit_copies(root_ref, unit, rows, x, y, is_left, to_ref, sems, base):
    few = rows // 4
    copies = []
    for k in range(2 * SIDE):
        row = rows_of(k, x, lax.bitwise_xor(y, 1), rows) + unit * few
        copies.append(
            pltpu.make_async_copy(
                root_ref.at[pl.ds(pl.multiple_of(row, few), few), :],
                to_ref.at[pl.ds(k * few, few), :],
                sems.at[base + k],
            )
        )
    return copies


def cross_copies(root_ref, unit, to_ref, sems, base):
    order = root_ref.shape[0]
    half, part = order // 2, order // 8
    return [
        pltpu.make_async_copy(
            root_ref.at[pl.ds((2 * unit + h) * part, part), pl.ds(half, half)],
            to_ref.at[:, pl.ds(h * half, half)],
            sems.at[base + h],
        )
        for h in range(2)
    ]


def column_of(owner_ref, pos, count):
    col = jnp.int32(0)
    for c in range(count):
        col = col + jnp.where(owner_ref[0, c] == pos, c, 0)
    return col


def position(x, y, d, j):
    return 2 * lax.bitwise_and(x + d, 3) + lax.bitwise_xor(lax.shift_right_logical(y, 1), j)


def cut(gradient, root, owner_table):
    rows, width = gradient.shape
    order = root.shape[0]
    count = width // order
    part = order // 8
    sizes = [(part + rows, order), (rows, order)] + [(2 * rows, order)] * 3

    def body(owner_ref, g_ref, root_ref, lead_ref, oth_ref, x1_ref, x2_ref, x3_ref, sems):
        x, y, is_left, outer = spot()
        outs = [(lead_ref.at[pl.ds(part, rows), :], oth_ref)]
        outs += [(r.at[pl.ds(0, rows), :], r.at[pl.ds(rows, rows), :]) for r in (x1_ref, x2_ref, x3_ref)]
        copies = []
        for d in range(SIDE):
            for j in range(2):
                col = column_of(owner_ref, position(x, y, d, j), count)
                at = pl.ds(pl.multiple_of(col * order, order), order)
                copies.append(pltpu.make_async_copy(g_ref.at[:, at], outs[d][j], sems.at[2 * d + j]))
        run(copies)
        chunk_ref = lead_ref.at[pl.ds(0, part), :]

        @pl.when(is_left)
        def _():
            finish(run(unit_copies(root_ref, 0, rows, x, y, is_left, chunk_ref, sems, 2 * SIDE)))

        @pl.when(jnp.logical_not(is_left))
        def _():
            finish(run(cross_copies(root_ref, 0, chunk_ref, sems, 2 * SIDE)))

        finish(copies)

    return call(
        body,
        [in_vmem(*size, dtype=jnp.float32) for size in sizes],
        [SMEM, HBM, HBM],
        [VMEM] * 5,
        [pltpu.SemaphoreType.DMA((4 * SIDE,))],
        0,
        8 * rows * width,
        60,
    )(owner_table, gradient, root)


def adam(gradient, moment, second, order):
    rows, width = gradient.shape
    count = width // order

    def body(g_ref, m_ref, s_ref, m_out, s_out, sums_ref):
        def step(i, total):
            at = pl.ds(pl.multiple_of(i * 8, 8), 8)
            g = g_ref[at, :]
            new_m = BETA_ONE * m_ref[at, :] + (1.0 - BETA_ONE) * g
            new_s = BETA_TWO * s_ref[at, :] + (1.0 - BETA_TWO) * g * g
            m_out[at, :] = new_m
            s_out[at, :] = new_s
            a = new_m / BIAS_ONE / (jnp.sqrt(new_s / BIAS_TWO) + ADAM_EPS)
            return total + a * a

        total = lax.fori_loop(0, rows // 8, step, jnp.zeros((8, 2 * order), jnp.float32))
        total = jnp.sum(total, axis=0, keepdims=True)
        for h in range(2):
            sums_ref[pl.ds(2 * pl.program_id(0) + h, 1), :] = total[:, h * order : (h + 1) * order]

    block = pl.BlockSpec((rows, 2 * order), lambda c: (0, c))
    return pl.pallas_call(
        body,
        grid=(count // 2,),
        out_shape=[f32(rows, width)] * 2 + [f32(8, order)],
        in_specs=[block] * 3,
        out_specs=[block] * 2 + [pl.BlockSpec((8, order), lambda c: (0, 0))],
        compiler_params=pltpu.CompilerParams(vmem_limit_bytes=40 * 2**20),
        cost_estimate=pl.CostEstimate(flops=0, bytes_accessed=24 * rows * width, transcendentals=0),
    )(gradient, moment, second)


def pack(root, rows):
    order = root.shape[0]
    half, quarter, part = order // 2, order // 4, order // 8

    def body(root_ref, b_ref, c_ref, buf, sems):
        x, y, is_left, outer = spot()
        places = [(b_ref, 0), (b_ref, part), (c_ref, 0)]
        b_ref[2 * part :, :] = jnp.zeros((8, order), jnp.float32)

        @pl.when(is_left)
        def _():
            copies = []
            for i in range(3):
                to_ref, first = places[i]
                to_ref = to_ref.at[pl.ds(first, part), :]
                copies += unit_copies(root_ref, i + 1, rows, x, y, is_left, to_ref, sems, 2 * SIDE * i)
            finish(run(copies))

        @pl.when(jnp.logical_not(is_left))
        def _():
            copies = cross_copies(root_ref, 1, b_ref.at[pl.ds(0, part), :], sems, 0)
            for i in range(2):
                at = pl.ds(i * half, half)
                copies.append(pltpu.make_async_copy(root_ref.at[at, at], buf.at[i], sems.at[2 + i]))
            finish(run(copies))
            row = lax.broadcasted_iota(jnp.int32, (quarter, quarter), 0)
            col = lax.broadcasted_iota(jnp.int32, (quarter, quarter), 1)
            for i in range(2):
                low = buf[i, quarter:, quarter:]
                both = jnp.where(row <= col, buf[i, :quarter, :quarter], low)
                out_ref, first = places[i + 1]
                at = slice(first, first + part)
                for h in range(2):
                    out_ref[at, h * half : h * half + quarter] = buf[i, h * part : (h + 1) * part, quarter:]
                    out_ref[at, h * half + quarter : (h + 1) * half] = both[h * part : (h + 1) * part]
                b_ref[2 * part + i : 2 * part + i + 1, :quarter] = jnp.sum(
                    jnp.where(row == col, low, 0.0), axis=0, keepdims=True
                )

    return call(
        body,
        [f32(2 * part + 8, order), f32(part, order)],
        [HBM],
        [VMEM, VMEM],
        [pltpu.VMEM((2, half, half), jnp.float32), pltpu.SemaphoreType.DMA((6 * SIDE,))],
        0,
        24 * part * order,
    )(root)


def in_vmem(*shape, dtype=jnp.bfloat16):
    return pltpu.VMEM(shape, dtype)


def cut_two(src, high, low, tiles):
    def step(i, carry):
        at = pl.ds(pl.multiple_of(i * 64, 64), 64)
        high[at, :], low[at, :] = split(src[at, :])
        return carry

    lax.fori_loop(0, tiles, step, 0)


def split_root(root, rows):
    order = root.shape[0]

    def body(root_ref, high_ref, low_ref, buf, sems):
        x, y, is_left, outer = spot()

        @pl.when(is_left)
        def _():
            copies = []
            for k in range(2 * SIDE):
                row = rows_of(k, x, y, rows)
                copies.append(
                    pltpu.make_async_copy(
                        root_ref.at[pl.ds(pl.multiple_of(row, rows), rows), :],
                        buf.at[pl.ds(k * rows, rows), :],
                        sems.at[k],
                    )
                )
            finish(run(copies))
            cut_two(buf, high_ref, low_ref, order // 128)

        @pl.when(jnp.logical_not(is_left))
        def _():
            finish(run([pltpu.make_async_copy(root_ref, buf, sems.at[0])]))
            cut_two(buf, high_ref, low_ref, order // 64)

    return call(
        body,
        [in_vmem(order, order)] * 2,
        [HBM],
        [VMEM, VMEM],
        [pltpu.VMEM((order, order), jnp.float32), pltpu.SemaphoreType.DMA((2 * SIDE,))],
        0,
        8 * order * order,
    )(root)


def first_product(pieces, rows, r_high, r_low):
    order = r_high.shape[0]
    half, tile = order // 2, order // 4
    count = len(pieces)

    def body(*refs):
        piece_refs, (rh_ref, rl_ref) = refs[:count], refs[count : count + 2]
        gh_ref, gl_ref, high_ref, low_ref, buf, sems = refs[count + 2 :]
        x, y, is_left, outer = spot()
        from_y = (y, 3 - y, lax.bitwise_xor(y, 1), 3 - lax.bitwise_xor(y, 1))
        copies = []
        for k in range(count):
            row = (lax.bitwise_and(x - k % SIDE, 3) * SIDE + from_y[k // SIDE]) * rows
            copies.append(
                pltpu.make_async_copy(
                    piece_refs[k].at[pl.ds(pieces[k][1], rows), :],
                    buf.at[pl.ds(pl.multiple_of(row, rows), rows), :],
                    sems.at[k],
                )
            )
        finish(run(copies))
        cut_two(buf, gh_ref, gl_ref, order // 64)

        def product(a_high, a_low, b_high, b_low, tiles):
            def step(i, carry):
                at = pl.ds(pl.multiple_of(i * tile, tile), tile)
                for n in range(2):
                    cols = slice(n * half, (n + 1) * half)
                    acc = mul_split(a_high[at, :], a_low[at, :], b_high[:, cols], b_low[:, cols])
                    high_ref[at, cols], low_ref[at, cols] = split(acc)
                return carry

            lax.fori_loop(0, tiles, step, 0)

        @pl.when(is_left)
        def _():
            product(rh_ref, rl_ref, gh_ref, gl_ref, 2)

        @pl.when(jnp.logical_not(is_left))
        def _():
            product(gh_ref, gl_ref, rh_ref, rl_ref, 4)

    return call(
        body,
        [in_vmem(order, order)] * 4,
        [HBM] * count + [VMEM] * 2,
        [VMEM] * 4,
        [pltpu.VMEM((order, order), jnp.float32), pltpu.SemaphoreType.DMA((count,))],
        0,
        order * order,
    )(*(piece for piece, _ in pieces), r_high, r_low)


def unfold(c_ref, first, diag, b_high, b_low, base):
    half = c_ref.shape[1] // 2
    quarter = half // 2
    mid = quarter // 2
    row = lax.broadcasted_iota(jnp.int32, (quarter, quarter), 0)
    col = lax.broadcasted_iota(jnp.int32, (quarter, quarter), 1)
    at = slice(first, first + mid)
    cross = jnp.concatenate([c_ref[at, :quarter], c_ref[at, half : half + quarter]], axis=0)
    both = jnp.concatenate([c_ref[at, quarter:half], c_ref[at, half + quarter :]], axis=0)
    turned = both.T
    top = jnp.where(row <= col, both, turned)
    low = jnp.where(row > col, both, jnp.where(row == col, diag, turned))
    for r, left_mat, right_mat in ((0, top, cross), (1, cross.T, low)):
        at = slice(base + r * quarter, base + (r + 1) * quarter)
        b_high[at, :quarter], b_low[at, :quarter] = split(left_mat)
        b_high[at, quarter:], b_low[at, quarter:] = split(right_mat)


def second_product(which, t_high, t_low, chunks, squares):
    order = t_high.shape[0]
    half, quarter, eighth = order // 2, order // 4, order // 8
    dests = 2 * SIDE
    part = quarter // dests
    few = part // 2
    count = len(chunks)

    def body(high_ref, low_ref, *refs):
        chunk_refs, sq_ref = refs[:count], refs[count]
        whole, sq_out, b_high, b_low = refs[count + 1 :]
        x, y, is_left, outer = spot()
        outs = []
        for k in range(dests):
            to_y = 3 - y if k % 2 else y
            outs.append(whole.at[2 * lax.bitwise_and(x + k // 2, 3) + lax.shift_right_logical(to_y, 1)])
        units = [(chunk_refs[0], 0), (chunk_refs[1], 0), (chunk_refs[1], eighth), (chunk_refs[-1], 0)]

        @pl.when(is_left)
        def _():
            for q in range(4):
                c_ref, first = units[q // 2]
                at = slice(q * eighth, (q + 1) * eighth)
                mat = c_ref[first : first + eighth, (q % 2) * half : (q % 2 + 1) * half]
                if which == 0:
                    b_high[half:, at], b_low[half:, at] = split(mat.T)
                else:
                    b_high[at, :], b_low[at, :] = split(mat)
            row = 2 * eighth + which
            diag = chunk_refs[1][row : row + 1, :quarter]
            unfold(*units[2 + which], diag, b_high, b_low, half * which)
            total = jnp.float32(0.0)
            for m in range(2):
                at = slice(m * quarter, (m + 1) * quarter)
                acc = mul_split(high_ref[at, :], low_ref[at, :], b_high[...], b_low[...])
                total = total + jnp.sum(acc * acc)
                for k in range(SIDE):
                    for h in range(2):
                        first = (2 * k + h) * part
                        for q in range(SIDE):
                            at = slice((h * SIDE + q) * part, (h * SIDE + q + 1) * part)
                            lanes = slice(q * 128, (q + 1) * 128)
                            outs[m * SIDE + k][at, :] = acc[first : first + part, lanes]
            sq_out[...] = sq_ref[...] + total

        @pl.when(jnp.logical_not(is_left))
        def _():
            mats = []
            for c_ref, first in units[2 * which : 2 * which + 2]:
                mats.append(c_ref[first : first + eighth, :])
            a_high, a_low = split(jnp.concatenate(mats, axis=0))
            total = jnp.float32(0.0)
            for n in range(2):
                cols = slice(n * half, (n + 1) * half)
                acc = mul_split(a_high, a_low, high_ref[:, cols], low_ref[:, cols])
                total = total + jnp.sum(acc * acc)
                for k in range(dests):
                    for q in range(SIDE):
                        first = (n * SIDE + q) * part
                        lanes = slice(q * 128, (q + 1) * 128)
                        outs[k][first : first + few, :] = acc[k * few : (k + 1) * few, lanes]
                        outs[k][first + few : first + part, :] = acc[
                            eighth + k * few : eighth + (k + 1) * few, lanes
                        ]
            sq_out[...] = sq_ref[...] + total

    short = pltpu.VMEM((order, half), jnp.bfloat16)
    return call(
        body,
        [pltpu.HBM((dests, 8 * part + 8 * which, 128), jnp.float32), f32(8, 128)],
        [VMEM] * (3 + count),
        [VMEM] * 2,
        [short, short],
        0,
        0,
        8,
    )(t_high, t_low, *chunks, squares)


def update_statistics(g_high, g_low, stat):
    order = g_high.shape[0]
    tile = order // 4
    tiles = order // tile

    def body(gh_ref, gl_ref, s_ref, out_ref, zero_ref, high, low):
        x, y, is_left, outer = spot()
        zero_ref[...] = jnp.zeros((8, 128), jnp.float32)

        @pl.when(is_left)
        def _():
            high[...] = gh_ref[...]
            low[...] = gl_ref[...]

        @pl.when(jnp.logical_not(is_left))
        def _():
            for i in range(tiles):
                for j in range(tiles):
                    at, cols = slice(i * tile, (i + 1) * tile), slice(j * tile, (j + 1) * tile)
                    high[at, cols] = gh_ref[cols, at].T
                    low[at, cols] = gl_ref[cols, at].T

        def outer_mul(a, b):
            return lax.dot_general(a, b, (((1,), (1,)), ((), ())), preferred_element_type=jnp.float32)

        for i in range(tiles):
            at = slice(i * tile, (i + 1) * tile)
            for j in range(i, tiles):
                to = slice(j * tile, (j + 1) * tile)
                acc = outer_mul(high[at, :], high[to, :]) + (
                    outer_mul(high[at, :], low[to, :]) + outer_mul(low[at, :], high[to, :])
                )
                acc = (1.0 - BETA_STAT) * acc
                out_ref[at, to] = BETA_STAT * s_ref[at, to] + acc
                if i != j:
                    out_ref[to, at] = BETA_STAT * s_ref[to, at] + acc.T

    short = pltpu.VMEM((order, order), jnp.bfloat16)
    return call(
        body,
        [f32(order, order), f32(8, 128)],
        [VMEM, VMEM, VMEM],
        [VMEM, VMEM],
        [short, short],
        0,
        order * order,
        14,
    )(g_high, g_low, stat)


def place_columns(first, second, sums, totals, owner_table, largest):
    count = first.shape[0]
    part = first.shape[1] // 8
    order = 8 * first.shape[2]
    end = 8 * part

    def body(owner_ref, first_ref, second_ref, sums_ref, totals_ref, out_ref, scratch):
        x, y, is_left, outer = spot()
        total = jnp.sum(jnp.sum(totals_ref[...], axis=0, keepdims=True), axis=1, keepdims=True)
        clip = jnp.minimum(1.0, largest / jnp.sqrt(total + 1e-06))
        scratch[...] = jnp.broadcast_to(jnp.sum(sums_ref[...], axis=1, keepdims=True), (count, 128))
        for c in range(count):
            p = owner_ref[0, c]
            from_left = (lax.bitwise_and(p, 1) == 0) == outer
            squares = second_ref[p, end : end + 1, :]
            scale = jnp.sqrt(scratch[c : c + 1, :] / (squares + 1e-06)) * clip
            for j in range(8):
                cols = slice(c * order + j * 128, c * order + (j + 1) * 128)
                at = slice(j * part, (j + 1) * part)
                back = (j + 4) % 8
                across = slice(back * part, (back + 1) * part)
                if j < 4:
                    out_ref[:part, cols] = first_ref[p, at, :] * scale
                    other = jnp.where(from_left, first_ref[p, across, :], second_ref[p, at, :])
                    out_ref[part:, cols] = other * scale
                else:
                    other = jnp.where(from_left, second_ref[p, across, :], first_ref[p, at, :])
                    out_ref[:part, cols] = other * scale
                    out_ref[part:, cols] = second_ref[p, at, :] * scale

    return call(
        body,
        f32(2 * part, count * order),
        [SMEM] + [VMEM] * 4,
        VMEM,
        [pltpu.VMEM((count, 128), jnp.float32)],
        0,
        16 * count * part * order,
    )(owner_table, first, second, sums, totals)


def with_squares(parts, squares, near_squares):
    rows = parts.shape[1]

    def body(parts_ref, squares_ref, near_ref, out_ref):
        for k in range(parts.shape[0]):
            out_ref[k] = squares_ref[...] + near_ref[...]

    return pl.pallas_call(
        body,
        grid=(1,),
        out_shape=f32(*parts.shape),
        in_specs=[pl.BlockSpec(memory_space=pl.ANY)] + [pl.BlockSpec((8, 128), lambda i: (0, 0))] * 2,
        out_specs=pl.BlockSpec((parts.shape[0], 8, 128), lambda i: (0, rows // 8 - 1, 0)),
        input_output_aliases={0: 0},
    )(parts, squares, near_squares)


def sent_back(parts):
    return lax.all_to_all(parts, "dp", 0, 0, axis_index_groups=GROUPS, tiled=True)


def local(gradient, moment, second, statistics, inv_roots, owner_table):
    rows_dev, width = gradient.shape
    order = statistics.shape[1]
    col_blocks = width // order
    root = inv_roots[0]

    lead, oth, x1, x2, x3 = cut(gradient, root, owner_table)
    lead_got = near(lead)
    far_y = {0: far(oth)}
    new_moment, new_second, own_sums = adam(gradient, moment, second, order)
    got_x = {1: along_x(x1, 1), 3: along_x(x3, 3)}
    got_x[2] = along_x(tie(x2, far_y[0], got_x[1], got_x[3], own_sums), 2)
    own_y = {d: got_x[d][:rows_dev] for d in (1, 2, 3)}
    oth_y = {d: got_x[d][rows_dev:] for d in (1, 2, 3)}
    for d in (1, 2, 3):
        far_y[d] = far(oth_y[d])

    chunk_b, chunk_c = pack(root, rows_dev)
    r_high, r_low = split_root(root, rows_dev)
    near_own = {1: near(tie(own_y[1], lead_got))}
    near_far = {0: near(tie(far_y[0], own_sums))}
    near_own[3] = near(tie(own_y[3], near_own[1], far_y[1], far_y[3]))
    near_far[1] = near(tie(far_y[1], near_far[0], got_x[2]))
    near_far[3] = near(tie(far_y[3], near_own[3]))
    near_own[2] = near(tie(own_y[2], near_far[1], far_y[2], chunk_b, chunk_c, r_high))
    near_far[2] = near(tie(far_y[2], near_far[3]))

    chunk_b = near(tie(chunk_b, near_own[2], near_far[2]))
    chunk_c = near(tie(chunk_c, near_own[2], near_far[2]))

    lead_rows = lead.shape[0] - rows_dev
    pieces = [(lead, lead_rows)] + [(got_x[d], 0) for d in (1, 2, 3)]
    pieces += [(far_y[d], 0) for d in range(SIDE)]
    pieces += [(lead_got, lead_rows)] + [(near_own[d], 0) for d in (1, 2, 3)]
    pieces += [(near_far[d], 0) for d in range(SIDE)]
    g_high, g_low, t_high, t_low = first_product(pieces, rows_dev, r_high, r_low)
    new_stat, squares = update_statistics(g_high, g_low, statistics[0])
    sums = tie(own_sums, squares)
    for bit in (4, 8):
        sums = sums + swap(sums, "dp", bit)
    squares = tie(squares, sums)
    half_a, squares = second_product(0, t_high, t_low, [lead_got, chunk_b], squares)
    sums = tie(sums, squares)
    sums = sums + swap(sums, "dp", 3)
    back_a = sent_back(tie(half_a, chunk_c, sums))
    half_b, squares = second_product(1, t_high, t_low, [lead_got, chunk_b, chunk_c], squares)
    near_squares = near(squares)
    totals = sums + swap(sums, "fsdp", 1)
    back_b = sent_back(tie(with_squares(half_b, tie(squares, totals), near_squares), back_a))
    totals = tie(totals, back_a)
    bit = 2
    while bit < lax.axis_size("fsdp"):
        totals = totals + swap(totals, "fsdp", bit)
        bit *= 2
    both = jnp.concatenate([sums, totals], axis=0)
    both = both + near(both)
    sums, totals = both[:col_blocks], both[col_blocks:]

    count_all = order * lax.axis_size("fsdp") * width
    update = place_columns(
        back_a, back_b, sums, totals, owner_table, CLIP_RMS * math.sqrt(count_all)
    )
    return (update, new_moment, new_second, new_stat[None])


def solution(mesh):
    placed = (
        P(("fsdp", "dp"), None),
        P(("fsdp", "dp"), None),
        P(("fsdp", "dp"), None),
        P(("fsdp", "dp"), None, None),
        P(("fsdp", "dp"), None, None),
        P("fsdp", None),
    )
    return jax.shard_map(
        local,
        mesh=mesh,
        in_specs=placed,
        out_specs=(
            P(("fsdp", "dp"), None),
            P(("fsdp", "dp"), None),
            P(("fsdp", "dp"), None),
            P(("fsdp", "dp"), None, None),
        ),
        check_vma=False,
    )
```
